256 devices in a mesh: section: 2 (over y_lo), head: 8 (over x, core), row: 16 (over z, y_hi).
Axes of the slice: x: 4, y: 4 (y_hi: 2, y_lo: 2; y = y_hi * 2 + y_lo), z: 8, core: 2. Of those that a mesh axis runs over, the one named last changes fastest.
Arguments:
- hidden: bfloat16 [2, 512, 8192], P('section', 'row'), may hold values from -6 to 6
- attn_gain: float32 [8192], replicated, may hold values from 0.1 to 1.9
- kv_weight: bfloat16 [8192, 2048], P(None, 'head'), may hold values from -0.0625 to 0.0625
- queries: bfloat16 [2, 512, 8192], P('section', 'row', 'head'), may hold values from -6 to 6
- cache_kv: bfloat16 [512, 768, 2048], P('row', None, 'head'), may hold values from -6 to 6
- lengths: int32 [512], P('row'), may hold values from 1 to 768, 196608 in all
- block_owner: int32 [128], replicated, may hold values from 0 to 511
- out_weight: bfloat16 [8192, 8192], P('head', 'row'), may hold values from -0.16572815 to 0.16572815
- final_gain: float32 [8192], replicated, may hold values from 0.1 to 1.9
- vocab_weight: bfloat16 [8192, 65536], P(None, ('section', 'head', 'row')), may hold values from -0.24 to 0.24
Outputs:
- layer_out: bfloat16 [2, 512, 8192], P('section', 'row')
- entropy: float32 [512], replicated
The draws below stay inside these ranges and needn't reach their ends.
Inputs may be any that keep to these rules, and one draw needn't show every extreme that they name: `lengths`: every draw has a row whose cache holds exactly 768 live positions.
All inputs are finite; a program needn't handle non-finite values. No bound on the sum of `lengths` on one device may be relied on, other than what follows from the above.
Results may differ from the reference program's by a relative error of at most 0.0055.
Values may be sent and summed in bfloat16 or wider, within the bound.
A program may use at most 128 MiB of HBM per device.

```python
import math
import jax
import jax.numpy as jnp
import numpy as np
from jax import lax

D = 8192
HD = 128
GROUP_Q = 8
VOCAB = 65536
BLK = 4
CACHE = 768
KVH = 8
QH = 64
ROWS = 512
NBLK = 128


def draw_queries(key, part):
    key = jax.random.fold_in(key, 3)
    base = jnp.clip(jax.random.normal(key, (2, ROWS, QH * HD), jnp.float32), -6.0, 6.0)
    return base.astype(jnp.bfloat16)


def draw_cache_kv(key, part):
    key = jax.random.fold_in(key, 5)
    base = jnp.clip(jax.random.normal(key, (ROWS, CACHE, KVH, 2, HD), jnp.float32), -6.0, 6.0)
    head_scale = jnp.exp(jax.random.uniform(jax.random.fold_in(key, 31), (KVH,), jnp.float32, -1.2, 1.0))
    part_scale = jnp.stack([jnp.ones((KVH,), jnp.float32), head_scale], axis=1)
    base = jnp.clip(base * part_scale[None, None, :, :, None], -6.0, 6.0)
    return base.reshape(ROWS, CACHE, KVH * 2 * HD).astype(jnp.bfloat16)


def draw_hidden(key, part):
    key = jax.random.fold_in(key, 7)
    base = jnp.clip(jax.random.normal(key, (2, ROWS, D), jnp.float32), -6.0, 6.0)
    base = base * jnp.array([1.0, 0.1], jnp.float32)[:, None, None]
    return base.astype(jnp.bfloat16)


def draw_out_weight(key, part):
    key = jax.random.fold_in(key, 13)
    base = jnp.clip(jax.random.normal(key, (QH, HD, D // 128, 128), jnp.float32), -6.0, 6.0)
    levels = jnp.exp(jax.random.uniform(jax.random.fold_in(key, 41), (QH, D // 128), jnp.float32, -1.5, 1.5)) / 1.8
    scaled = base * levels[:, None, :, None] / math.sqrt(QH * HD)
    return scaled.reshape(QH * HD, D).astype(jnp.bfloat16)


def draw_vocab_weight(key, part):
    key = jax.random.fold_in(key, 9)
    spread = 3.0 / math.sqrt(D)
    base = jnp.clip(spread * jax.random.normal(key, (D, VOCAB), jnp.float32), -6.0 * spread, 6.0 * spread)
    return base.astype(jnp.bfloat16)


def touch_ends(result, key, low, top_value):
    spot = [jax.random.randint(jax.random.fold_in(key, axis), (), 0, length) for axis, length in enumerate(result.shape)]
    main_axis = result.shape.index(max(result.shape))
    next_to = spot[:main_axis] + [(spot[main_axis] + 1) % result.shape[main_axis]] + spot[main_axis + 1:]
    return result.at[tuple(spot)].set(low).at[tuple(next_to)].set(top_value)


def block_levels(stream_key, shape, cuts, smallest, top_value):
    factor_of = 1.0
    for dim, shards_of in cuts:
        heights = jax.random.uniform(jax.random.fold_in(jax.random.fold_in(stream_key, 6), dim), (shards_of,), jnp.float32, smallest / len(cuts), top_value / len(cuts))
        factor_of = factor_of * jnp.repeat(jnp.exp(heights), shape[dim] // shards_of).reshape((-1,) + (1,) * (len(shape) - 1 - dim))
    return factor_of


def profile(number_of, total, bound, slope):
    weights = [(1 << 20) // math.isqrt(grade ** slope) + 1 for grade in range(2, number_of + 1)]
    surplus, holding = total - bound - (number_of - 1), [1] * (number_of - 1)
    while surplus > 0:
        movable = [i for i in range(number_of - 1) if holding[i] < bound]
        pool, budget = sum([weights[i] for i in movable]), surplus
        for i in movable:
            extra = min(bound - holding[i], max(1, budget * weights[i] // pool), surplus)
            holding[i] = holding[i] + extra
            surplus = surplus - extra
    return np.array([bound] + holding)


def uneven(stream_key, number_of, total, limit, slope):
    if number_of == 2:
        one = jax.random.randint(stream_key, (), max(1, total - limit), min(limit, total - 1) + 1)
        return jnp.stack([one, total - one])
    sizes = jnp.asarray(profile(number_of, total, limit, slope), jnp.int32)
    twos = (number_of - 1) // 2
    source_of, taker = sizes[1:1 + 2 * twos:2], sizes[2:2 + 2 * twos:2]
    slack = jnp.minimum(source_of - 1, limit - taker)
    moved = jax.random.randint(jax.random.fold_in(stream_key, 1), (twos,), 0, 1 << 20) % (slack + 1)
    sizes = sizes.at[1:1 + 2 * twos:2].set(source_of - moved).at[2:2 + 2 * twos:2].set(taker + moved)
    return sizes[jax.random.permutation(jax.random.fold_in(stream_key, 2), number_of)]


def gaussian(own_key, dims, deviation, most, split=(), kind=jnp.bfloat16):
    drawn = jax.random.normal(own_key, dims, jnp.float32) * deviation
    if len(split) > 0:
        drawn = block_levels(own_key, dims, split, -0.22, 0.18) * drawn
    return jnp.clip(drawn, min=-most, max=most).astype(kind)


def setup_inputs(seed: int = 0) -> dict:
    splits = jax.random.split(jax.random.key(seed), 11)
    return {
        "hidden": draw_hidden(jax.random.fold_in(splits[10], 71), 0),
        "attn_gain": jnp.clip(1.0 + 0.18 * jax.random.normal(splits[1], (D,), jnp.float32), 0.1, 1.9),
        "kv_weight": gaussian(splits[2], (D, KVH * 2 * HD), D ** -0.5, 0.0625, ((1, 8),)),
        "queries": draw_queries(jax.random.fold_in(splits[10], 71), 0),
        "cache_kv": draw_cache_kv(jax.random.fold_in(splits[10], 71), 0),
        "lengths": uneven(splits[5], ROWS, ROWS * CACHE // 2, CACHE, 2).astype(jnp.int32),
        "block_owner": touch_ends(jax.random.randint(splits[6], (NBLK,), 0, ROWS), jax.random.fold_in(splits[6], 1), 0, ROWS - 1).astype(jnp.int32),
        "out_weight": draw_out_weight(jax.random.fold_in(splits[10], 71), 0),
        "final_gain": jnp.clip(1.0 + 0.18 * jax.random.normal(splits[8], (D,), jnp.float32), 0.1, 1.9),
        "vocab_weight": draw_vocab_weight(jax.random.fold_in(splits[10], 71), 0),
    }


NORM_EPSILON = 1e-05

def rms_scale(values, gain):
    wide = values.astype(jnp.float32)
    spread = lax.optimization_barrier(jnp.mean(wide * wide, axis=-1, keepdims=True))
    return wide * lax.rsqrt(spread + NORM_EPSILON) * gain

def round_trip(values):
    return lax.optimization_barrier(values.astype(jnp.bfloat16)).astype(jnp.float32)

def reference(hidden, attn_gain, kv_weight, queries, cache_kv, lengths, block_owner, out_weight, final_gain, vocab_weight):
    score_scale = 1.0 / math.sqrt(HD)
    normed = rms_scale(hidden, attn_gain).astype(jnp.bfloat16)
    fresh_kv = jnp.dot(normed.reshape(2 * ROWS, D), kv_weight, preferred_element_type=jnp.float32)
    fresh_kv = fresh_kv.astype(jnp.bfloat16).astype(jnp.float32).reshape(2, ROWS, KVH, 2, HD)
    prompt_keys = fresh_kv[0, :, :, 0]
    prompt_vals = fresh_kv[0, :, :, 1]
    own_keys = fresh_kv[1, :, :, 0]
    own_vals = fresh_kv[1, :, :, 1]
    asked_rows = queries.astype(jnp.float32).reshape(2, ROWS, KVH, GROUP_Q, HD)
    position = jnp.arange(ROWS, dtype=jnp.int32)
    causal = position[None, :] <= position[:, None]
    first_scores = jnp.einsum('ihgd,thd->ihgt', asked_rows[0], prompt_keys) * score_scale
    first_scores = jnp.where(causal[:, None, None, :], first_scores, -jnp.inf)
    top_score = lax.optimization_barrier(jnp.max(first_scores, axis=-1, keepdims=True))
    weights = jnp.exp(first_scores - top_score)
    weight_sum = lax.optimization_barrier(jnp.sum(weights, axis=-1))
    prefill_out = jnp.einsum('ihgt,thd->ihgd', round_trip(weights), prompt_vals) / weight_sum[..., None]
    cache = cache_kv.reshape(ROWS, CACHE, KVH, 2, HD)
    cache_keys = cache[:, :, :, 0].astype(jnp.float32)
    cache_vals = cache[:, :, :, 1].astype(jnp.float32)
    asked_dec = asked_rows[1]
    cache_scores = jnp.einsum('jhgd,jchd->jhgc', asked_dec, cache_keys) * score_scale
    live = jnp.arange(CACHE, dtype=jnp.int32)[None, :] < lengths[:, None]
    cache_scores = jnp.where(live[:, None, None, :], cache_scores, -jnp.inf)
    owners = jnp.repeat(block_owner, BLK)
    owned = owners[None, :] == position[:, None]
    block_scores = jnp.einsum('jhgd,thd->jhgt', asked_dec, prompt_keys) * score_scale
    block_scores = jnp.where(owned[:, None, None, :], block_scores, -jnp.inf)
    own_scores = jnp.einsum('jhgd,jhd->jhg', asked_dec, own_keys) * score_scale
    top_score = jnp.maximum(jnp.maximum(lax.optimization_barrier(jnp.max(cache_scores, axis=-1)), lax.optimization_barrier(jnp.max(block_scores, axis=-1))), own_scores)
    cache_weights = jnp.exp(cache_scores - top_score[..., None])
    block_weights = jnp.exp(block_scores - top_score[..., None])
    own_weights = jnp.exp(own_scores - top_score)
    weight_sum = lax.optimization_barrier(jnp.sum(cache_weights, axis=-1)) + lax.optimization_barrier(jnp.sum(block_weights, axis=-1)) + own_weights
    gathered = jnp.einsum('jhgc,jchd->jhgd', round_trip(cache_weights), cache_vals)
    gathered = gathered + jnp.einsum('jhgt,thd->jhgd', round_trip(block_weights), prompt_vals)
    gathered = gathered + round_trip(own_weights)[..., None] * own_vals[:, :, None, :]
    decode_out = gathered / weight_sum[..., None]
    attention = jnp.stack([prefill_out, decode_out]).astype(jnp.bfloat16).reshape(2 * ROWS, QH * HD)
    projected = jnp.dot(attention, out_weight, preferred_element_type=jnp.float32).reshape(2, ROWS, D)
    layer_out = (hidden.astype(jnp.float32) + projected).astype(jnp.bfloat16)
    final_rows = rms_scale(layer_out[1], final_gain).astype(jnp.bfloat16)
    logits = jnp.dot(final_rows, vocab_weight, preferred_element_type=jnp.float32)
    top_logit = lax.optimization_barrier(jnp.max(logits, axis=1, keepdims=True))
    shifted = logits - top_logit
    exponent_terms = jnp.exp(shifted)
    total_mass = lax.optimization_barrier(jnp.sum(exponent_terms, axis=1))
    moment = lax.optimization_barrier(jnp.sum(exponent_terms * shifted, axis=1))
    entropy = jnp.log(total_mass) - moment / total_mass
    return (layer_out, entropy)
```

```python
import functools
import math

import jax
import jax.numpy as jnp
from jax import lax
from jax.experimental import pallas as pl
from jax.experimental.pallas import tpu as pltpu
from jax.sharding import PartitionSpec as P

MESH = pl.DeviceIdType.MESH
BF = jnp.bfloat16
F32 = jnp.float32
EPS = 1e-05
NEG = -1e30
BLK = 4
NX, NY, NZ = 4, 4, 8
TOK = 32
COLS = 1024
CACHE_PARTS = 8
KV_PARTS = 4


def dot(a, b):
    return jnp.dot(a, b, preferred_element_type=F32)


def dot_t(a, b):
    return lax.dot_general(a, b, (((1,), (1,)), ((), ())), preferred_element_type=F32)


def wrap(value, n):
    return lax.rem(value + n, n)


class Place:
    def __init__(self):
        s, h, r = (lax.axis_index(a) for a in ("section", "head", "row"))
        self.s, self.h, self.r = s, h, r
        self.x, self.c = lax.div(h, 2), lax.rem(h, 2)
        self.z, self.yh = lax.div(r, 2), lax.rem(r, 2)
        self.y = self.yh * 2 + s
        self.decode = s == 1
        self.prefill = s == 0

    def at(self, x, y, z, c):
        return (lax.rem(y, 2), x * 2 + c, z * 2 + lax.div(y, 2))

    def off(self, dx=0, dy=0, dz=0, dc=0):
        x = wrap(self.x + dx, NX) if dx else self.x
        y = wrap(self.y + dy, NY) if dy else self.y
        z = wrap(self.z + dz, NZ) if dz else self.z
        c = 1 - self.c if dc else self.c
        return self.at(x, y, z, c)


def remote(src, dst, ssem, rsem, device):
    return pltpu.make_async_remote_copy(
        src_ref=src, dst_ref=dst, send_sem=ssem, recv_sem=rsem,
        device_id=device, device_id_type=MESH,
    )


def ring4(me, axis, block, half, ssem, rsem, late):
    at = me.x if axis == "dx" else me.y

    def copy(k):
        if k < 2:
            ref = block(at)
        else:
            ref = half(wrap(at - 1 if k == 2 else at + 1, 4), k - 2)
        to = me.off(**{axis: 1 if k in (0, 2) else -1})
        return remote(ref, ref, ssem.at[k], rsem.at[k], to)

    def arrived(k):
        if k == 0:
            ref = block(wrap(at - 1, 4))
        elif k == 1:
            ref = block(wrap(at + 1, 4))
        else:
            ref = half(wrap(at + 2, 4), k - 2)
        return remote(ref, ref, ssem.at[k], rsem.at[k], me.off(**{axis: 1}))

    copy(0).start()
    copy(1).start()
    yield
    arrived(0).wait_recv()
    copy(2).start()
    arrived(1).wait_recv()
    copy(3).start()
    yield
    arrived(2).wait_recv()
    arrived(3).wait_recv()
    for k in range(4):
        late.append(functools.partial(copy, k))


def ring8(me, block, half, ssem, rsem, late):
    z = me.z

    def copy(d, k):
        origin = wrap(z - k, NZ) if d == 0 else wrap(z + k, NZ)
        ref = block(origin) if k < 3 else half(origin, d)
        return remote(ref, ref, ssem.at[d, k], rsem.at[d, k], me.off(dz=1 - 2 * d))

    def arrived(d, k):
        origin = wrap(z - 1 - k, NZ) if d == 0 else wrap(z + 1 + k, NZ)
        ref = block(origin) if k < 3 else half(origin, d)
        return remote(ref, ref, ssem.at[d, k], rsem.at[d, k], me.off(dz=1 - 2 * d))

    copy(0, 0).start()
    copy(1, 0).start()
    for k in range(1, 4):
        yield
        for d in range(2):
            arrived(d, k - 1).wait_recv()
            copy(d, k).start()
    yield
    for d in range(2):
        arrived(d, 3).wait_recv()
    for k in range(4):
        for d in range(2):
            late.append(functools.partial(copy, d, k))


def only(flag, steps):
    going = True
    while going:
        box = []

        @pl.when(flag)
        def _():
            box.append(next(steps, "end"))

        going = box[0] != "end"
        if going:
            yield


def spread_y(me, block, half, ssem, rsem, late):
    up, down = me.off(dy=1), me.off(dy=-1)
    yh = me.yh

    def pair(ref, k, to):
        return remote(ref, ref, ssem.at[k], rsem.at[k], to)

    @pl.when(me.decode)
    def _():
        pair(block(yh), 0, up).start()
        pair(block(yh), 1, down).start()

    yield

    @pl.when(me.prefill)
    def _():
        pair(block(1 - yh), 0, up).wait_recv()
        pair(half(1 - yh, 0), 2, up).start()
        pair(block(yh), 1, up).wait_recv()
        pair(half(yh, 1), 3, down).start()

    yield

    @pl.when(me.decode)
    def _():
        pair(half(1 - yh, 0), 2, up).wait_recv()
        pair(half(1 - yh, 1), 3, up).wait_recv()
        pair(block(yh), 0, up).wait_send()
        pair(block(yh), 1, down).wait_send()

    @pl.when(me.prefill)
    def _():
        pair(half(1 - yh, 0), 2, up).wait_send()
        pair(half(yh, 1), 3, down).wait_send()


def kernel(
    hid, again, q, lens, owners, fgain, kvw_h, cache_h, wout_h, vocab_h,
    lay, ent,
    kvw, cache, wv, vv, kvbuf, qs, m1, l1, o1, abuf, psend, precv, xs, xr, own, hpart,
    ga, gb, gc, acc, ssq, st1, st2, mine,
    lsem, csem, kvs_sem, kvr_sem, wsem, hs_sem, hr_sem, as_sem, ar_sem, ps_sem, xs_sem, xr_sem,
    p4s, p4r, p8s, p8r, pys, pyr, ls_sem, lr_sem, t1s, t1r, t2s, t2r, es_sem,
):
    me = Place()
    decode, prefill = me.decode, me.prefill
    x, y, z, c, yh, h, r = me.x, me.y, me.z, me.c, me.yh, me.h, me.r
    d_model = hid.shape[1]
    late = []

    cache_copies = [
        pltpu.make_async_copy(
            cache_h.at[pl.ds(i * 4, 4)], cache.at[pl.ds(i * 4, 4)], csem.at[i]
        )
        for i in range(CACHE_PARTS)
    ]
    step = d_model // KV_PARTS
    kv_copies = [
        pltpu.make_async_copy(
            kvw_h.at[pl.ds(i * step, step)], kvw.at[pl.ds(i * step, step)], lsem.at[i]
        )
        for i in range(KV_PARTS)
    ]
    w_copy = pltpu.make_async_copy(wout_h, wv.at[yh], lsem.at[KV_PARTS])
    v_copy = pltpu.make_async_copy(vocab_h, vv.at[0], lsem.at[KV_PARTS + 1])

    @pl.when(decode)
    def _():
        for cp in cache_copies:
            cp.start()

    for cp in kv_copies:
        cp.start()
    w_copy.start()
    v_copy.start()

    peers = [dict(dz=k) for k in range(1, NZ)]
    peers += [dict(dy=2, dz=k) for k in range(1, NZ)]
    peers += [dict(dx=i, dy=j) for i in range(NX) for j in range(NY) if i or j]
    peers += [dict(dc=1)]
    barrier = pltpu.get_barrier_semaphore()
    for p in peers:
        pl.semaphore_signal(barrier, 1, device_id=me.off(**p), device_id_type=MESH)
    pl.semaphore_wait(barrier, len(peers))

    vocab_swap = remote(vocab_h, vv.at[1], wsem.at[0], wsem.at[1], me.off(dc=1))
    vocab_swap.start()
    near = wrap(jnp.where(decode, y + 1, y - 1), NY)
    w_swap = remote(wout_h, wv.at[yh], wsem.at[2], wsem.at[3], me.at(x, near, z, c))
    w_swap.start()
    w_swapped = remote(wout_h, wv.at[1 - yh], wsem.at[2], wsem.at[3], me.at(x, near, z, c))

    def hidden_part(to):
        return hid.at[:, pl.ds(pl.multiple_of(to * COLS, COLS), COLS)]

    @pl.when(z == h)
    def _():
        for k in range(1, NZ):
            to = wrap(z + k, NZ)
            remote(hidden_part(to), hpart, hs_sem.at[k], hr_sem, me.at(x, y, to, c)).start()
        hpart[...] = hid[:, pl.ds(pl.multiple_of(z * COLS, COLS), COLS)]

    for g in range(8):
        qs[pl.ds(g, TOK, stride=8), :] = q[:, g * 128:(g + 1) * 128].astype(F32)
    scale = 1.0 / math.sqrt(128)

    @pl.when(prefill)
    def _():
        m1[...] = jnp.full_like(m1, NEG)
        l1[...] = jnp.zeros_like(l1)
        o1[...] = jnp.zeros_like(o1)

    @pl.when(decode)
    def _():
        cache_len = cache.shape[1]

        def rows(first):
            parts = []
            for j in range(4):
                i = first + j
                qi = qs[pl.ds(pl.multiple_of(i * 8, 8), 8), :].astype(BF)
                s = dot_t(qi, cache[i, :, 0:128]) * scale
                at = lax.broadcasted_iota(jnp.int32, (8, cache_len), 1)
                parts.append(jnp.where(at < lens[i], s, NEG))
            s = jnp.concatenate(parts, axis=0)
            top = jnp.max(s, axis=1, keepdims=True)
            p = jnp.exp(s - top)
            total = jnp.sum(p, axis=1, keepdims=True)
            pb = p.astype(BF)
            where = pl.ds(pl.multiple_of(first * 8, 32), 32)
            m1[where, :] = jnp.broadcast_to(top, (32, 128))
            l1[where, :] = jnp.broadcast_to(total, (32, 128))
            out = [dot(pb[8 * j:8 * j + 8], cache[first + j, :, 128:256]) for j in range(4)]
            o1[where, :] = jnp.concatenate(out, axis=0)

        for i in range(CACHE_PARTS):
            cache_copies[i].wait()
            rows(i * 4)

    def square(i, total):
        w = hid[:, pl.ds(pl.multiple_of(i * 1024, 1024), 1024)].astype(F32)
        return total + jnp.sum(w * w, axis=1, keepdims=True)

    total = lax.fori_loop(0, d_model // 1024, square, jnp.zeros((TOK, 1), F32))
    inv = lax.rsqrt(total / d_model + EPS)
    fresh = jnp.zeros((TOK, 256), F32)
    for i in range(KV_PARTS):
        kv_copies[i].wait()

        def part(j, sum_, i=i):
            at = pl.ds(pl.multiple_of(i * step + j * 512, 512), 512)
            n = (hid[:, at].astype(F32) * inv * again[:, at]).astype(BF)
            return sum_ + dot(n, kvw[at, :])

        fresh = lax.fori_loop(0, step // 512, part, fresh)
    fresh = fresh.astype(BF)

    up, down = me.off(dy=1), me.off(dy=-1)

    def kv_block(zz, hh):
        return kvbuf.at[zz * 2 + hh]

    @pl.when(prefill)
    def _():
        kvbuf[r] = fresh
        sent = []
        order = [(0, 1)] + [(k, j) for k in (1, 7, 2, 6, 3, 5, 4) for j in (0, 1)]
        for n, (k, j) in enumerate(order):
            cp = remote(kvbuf.at[r], kvbuf.at[r], kvs_sem.at[n], kvr_sem.at[r],
                        me.off(dz=k, dy=2 * j))
            cp.start()
            sent.append(cp)
        n = 15
        for k in (0, 1, 7, 2, 6, 3, 5, 4):
            zz = wrap(z + k, NZ)
            ref, sem = kv_block(zz, yh), kvr_sem.at[zz * 2 + yh]
            if k:
                remote(ref, ref, kvs_sem.at[n], sem, up).wait_recv()
            for to in (up, down):
                cp = remote(ref, ref, kvs_sem.at[n], sem, to)
                cp.start()
                sent.append(cp)
                n += 1
        for k in range(NZ):
            zz = wrap(z + k, NZ)
            ref, sem = kv_block(zz, 1 - yh), kvr_sem.at[zz * 2 + 1 - yh]
            remote(ref, ref, kvs_sem.at[0], sem, up).wait_recv()
        for cp in sent:
            cp.wait_send()

    @pl.when(decode)
    def _():
        for i in range(16):
            remote(kvbuf.at[i], kvbuf.at[i], kvs_sem.at[0], kvr_sem.at[i], up).wait_recv()

    keys = kvbuf[:, :, 0:128].reshape(16 * TOK, 128)
    vals = kvbuf[:, :, 128:256].reshape(16 * TOK, 128)
    own_key = fresh[:, 0:128].astype(F32)
    own_val = fresh[:, 128:256].astype(F32)
    slot = c_slot(z)
    flag = jnp.where(decode, 1, 0)
    for half in range(2):
        heads = range(half * 4, half * 4 + 4)
        qh = jnp.concatenate([q[:, g * 128:(g + 1) * 128] for g in heads], axis=0)
        s = dot_t(qh, keys) * scale
        row = r * TOK + lax.rem(lax.broadcasted_iota(jnp.int32, s.shape, 0), TOK)
        tok = lax.broadcasted_iota(jnp.int32, s.shape, 1)
        off = flag * jnp.abs(owners[...] - row) + (1 - flag) * jnp.maximum(tok - row, 0)
        s = jnp.where(off == 0, s, NEG)
        mc = jnp.concatenate([m1[pl.ds(g, TOK, stride=8), :] for g in heads], axis=0)
        lc = jnp.concatenate([l1[pl.ds(g, TOK, stride=8), :] for g in heads], axis=0)
        oc = jnp.concatenate([o1[pl.ds(g, TOK, stride=8), :] for g in heads], axis=0)
        ok = jnp.concatenate([own_key] * 4, axis=0)
        ov = jnp.concatenate([own_val] * 4, axis=0)
        so = jnp.sum(qh.astype(F32) * ok, axis=1, keepdims=True) * scale
        so = jnp.where(jnp.broadcast_to(flag, so.shape) == 1, so, NEG)
        mc, lc = mc[:, 0:1], lc[:, 0:1]
        top = jnp.maximum(jnp.maximum(jnp.max(s, axis=1, keepdims=True), mc), so)
        p = jnp.exp(s - top)
        fac = jnp.exp(mc - top)
        po = jnp.exp(so - top)
        total = jnp.sum(p, axis=1, keepdims=True) + lc * fac + po
        out = dot(p.astype(BF), vals) + oc * fac + po.astype(BF).astype(F32) * ov
        out = (out / total).astype(BF)
        for j, g in enumerate(heads):
            abuf[slot, :, g * 128:(g + 1) * 128] = out[j * TOK:(j + 1) * TOK]

    drain(ring8(
        me,
        lambda zz: abuf.at[c_slot(zz)],
        lambda zz, k: abuf.at[c_slot(zz), pl.ds(k * 16, 16)],
        as_sem, ar_sem, late,
    ))

    w_copy.wait()
    w_swapped.wait_recv()
    half_cols = COLS // 2

    def project(parity):
        rows = abuf[pl.ds(parity * 4, 4)].reshape(4 * TOK, COLS)
        return [dot(rows, wv[j]) for j in range(2)]

    for j, v in enumerate(project(1 - c)):
        psend[:, :, j * half_cols:(j + 1) * half_cols] = v.astype(BF).reshape(4, TOK, half_cols)
    swap = remote(psend, precv, ps_sem.at[0], ps_sem.at[1], me.off(dc=1))
    swap.start()
    mine_sum = project(c)
    swap.wait_recv()
    total = []
    for j in range(2):
        v = mine_sum[j].reshape(4, TOK, half_cols)
        v = v + precv[:, :, j * half_cols:(j + 1) * half_cols].astype(F32)
        xs[:, :, j * half_cols:(j + 1) * half_cols] = v.astype(BF)
        for i in range(4):
            @pl.when(x == i)
            def _(v=v, i=i, j=j):
                own[:, j * half_cols:(j + 1) * half_cols] = v[i]

    sends = []
    for k in (1, 3, 2):
        to = wrap(x + k, NX)
        cp = remote(xs.at[to], xr.at[k - 1], xs_sem.at[k - 1], xr_sem.at[k - 1], me.at(to, y, z, c))
        cp.start()
        sends.append(cp)

    @pl.when(z != h)
    def _():
        remote(hpart, hpart, hs_sem.at[0], hr_sem, up).wait_recv()

    for cp in sends:
        cp.wait_recv()
    rows_out = own[...] + hpart[...].astype(F32)
    for k in range(3):
        rows_out = rows_out + xr[k].astype(F32)
    mine[...] = rows_out.astype(BF)
    col0 = pl.multiple_of(z * COLS, COLS)

    @pl.when(decode)
    def _():
        ga[z, yh, x] = mine[0:16, 0:half_cols]
        gc[yh, z, x] = mine[0:16, half_cols:COLS]
        gb[x, yh, z] = mine[16:32, :]

    def columns_of(zz):
        return lay.at[:, pl.ds(pl.multiple_of(zz * COLS, COLS), COLS)]

    home = me.at(x, y, h, c)

    @pl.when(prefill & (z != h))
    def _():
        remote(mine, columns_of(z), ls_sem.at[0], lr_sem.at[z], home).start()

    def part_a():
        yield from only(decode, ring4(
            me, "dx", lambda i: ga.at[z, yh, i], lambda i, k: ga.at[z, yh, i, :, pl.ds(k * 256, 256)],
            p4s.at[0], p4r.at[0], late_decode))
        yield from spread_y(
            me, lambda i: ga.at[z, i], lambda i, k: ga.at[z, i, pl.ds(2 * k, 2)],
            pys.at[0], pyr.at[0], late)
        yield from ring8(
            me, lambda i: ga.at[i], lambda i, k: ga.at[i, k], p8s.at[0], p8r.at[0], late)

    def part_c():
        yield from only(decode, ring4(
            me, "dx", lambda i: gc.at[yh, z, i], lambda i, k: gc.at[yh, z, i, :, pl.ds(k * 256, 256)],
            p4s.at[1], p4r.at[1], late_decode))
        yield from only(decode, ring8(
            me, lambda i: gc.at[yh, i], lambda i, k: gc.at[yh, i, pl.ds(2 * k, 2)],
            p8s.at[1], p8r.at[1], late_decode))
        yield from spread_y(
            me, lambda i: gc.at[i], lambda i, k: gc.at[i, pl.ds(4 * k, 4)],
            pys.at[1], pyr.at[1], late)

    def part_b():
        yield from only(decode, ring8(
            me, lambda i: gb.at[x, yh, i], lambda i, k: gb.at[x, yh, i, :, pl.ds(k * 512, 512)],
            p8s.at[2], p8r.at[2], late_decode))
        yield from spread_y(
            me, lambda i: gb.at[x, i], lambda i, k: gb.at[x, i, pl.ds(4 * k, 4)],
            pys.at[2], pyr.at[2], late)
        yield from ring4(
            me, "dx", lambda i: gb.at[i], lambda i, k: gb.at[i, k], p4s.at[2], p4r.at[2], late)

    late_decode = []
    drain(part_b(), part_a(), part_c())

    holder = c == lax.rem(z, 2)
    xz = lax.div(z, 2)
    source = holder & (x == xz)

    @pl.when(decode & holder)
    def _():
        for zz in range(NZ):
            lay[0:16, zz * COLS:zz * COLS + half_cols] = ga[zz, yh, xz]
            lay[0:16, zz * COLS + half_cols:(zz + 1) * COLS] = gc[yh, zz, xz]
            lay[16:32, zz * COLS:(zz + 1) * COLS] = gb[xz, yh, zz]

    @pl.when(prefill & source)
    def _():
        for k in range(1, NZ):
            zz = wrap(z + k, NZ)
            remote(mine, columns_of(zz), ls_sem.at[0], lr_sem.at[zz], home).wait_recv()
        lay[:, pl.ds(col0, COLS)] = mine[...]
        for k in (1, 3, 2):
            remote(lay, lay, ls_sem.at[k], lr_sem.at[NZ], me.off(dx=k)).start()

    @pl.when(prefill & holder & (x != xz))
    def _():
        remote(lay, lay, ls_sem.at[1], lr_sem.at[NZ], up).wait_recv()

    core_copy = remote(lay, lay, ls_sem.at[4], lr_sem.at[NZ + 1], me.off(dc=1))

    @pl.when(holder)
    def _():
        core_copy.start()

    v_copy.wait()
    vocab_swap.wait_recv()
    acc[...] = jnp.zeros_like(acc)
    ssq[...] = jnp.zeros_like(ssq)

    def block(zz, carry):
        base = pl.multiple_of(zz * COLS, COLS)
        for j in range(2):
            lo = (ga[zz] if j == 0 else gc[:, zz]).reshape(128, half_cols)
            hi = gb[:, :, zz, :, j * half_cols:(j + 1) * half_cols].reshape(128, half_cols)
            rows = jnp.concatenate([lo, hi], axis=0).astype(F32)
            at = pl.ds(base + j * half_cols, half_cols)
            sq = rows * rows
            ssq[...] += sq[:, 0:128] + sq[:, 128:256] + sq[:, 256:384] + sq[:, 384:512]
            gained = (rows * fgain[:, at]).astype(BF)
            for k in range(2):
                acc[:, k * 256:(k + 1) * 256] += dot(gained, vv[k, at, :])
        return carry

    lax.fori_loop(0, NZ, block, 0)
    inv = lax.rsqrt(jnp.sum(ssq[...], axis=1, keepdims=True) / d_model + EPS)
    logits = acc[...] * inv
    top = jnp.max(logits, axis=1, keepdims=True)
    shifted = logits - top
    e = jnp.exp(shifted)
    mass = jnp.sum(e, axis=1, keepdims=True)
    moment = jnp.sum(e * shifted, axis=1, keepdims=True)
    lane = lax.broadcasted_iota(jnp.int32, (256, 128), 1)
    packed = jnp.where(lane == 0, top, jnp.where(lane == 1, mass, moment))
    here = x * NY + y
    st1[here] = jnp.transpose(packed)[0:8]

    def merge(ref, n):
        tops = [ref[i, 0:1, :] for i in range(n)]
        best = tops[0]
        for t in tops[1:]:
            best = jnp.maximum(best, t)
        mass = jnp.zeros_like(best)
        moment = jnp.zeros_like(best)
        for i in range(n):
            gap = tops[i] - best
            f = jnp.exp(gap)
            mass = mass + f * ref[i, 1:2, :]
            moment = moment + f * (ref[i, 2:3, :] + gap * ref[i, 1:2, :])
        return best, mass, moment

    sent = []
    for i in range(NX):
        for j in range(NY):
            n = i * NY + j
            if n:
                cp = remote(st1.at[here], st1.at[here], t1s.at[n], t1r.at[here], me.off(dx=i, dy=j))
                cp.start()
                sent.append(cp)
    for i in range(NX):
        for j in range(NY):
            if i or j:
                n = wrap(x + i, NX) * NY + wrap(y + j, NY)
                remote(st1.at[n], st1.at[n], t1s.at[0], t1r.at[n], up).wait_recv()
    best, mass, moment = merge(st1, 16)
    st2[z, 0:1, :] = best
    st2[z, 1:2, :] = mass
    st2[z, 2:3, :] = moment
    sent2 = []
    for k in (4, 3, 5, 2, 6, 1, 7):
        cp = remote(st2.at[z], st2.at[z], t2s.at[k], t2r.at[z], me.off(dz=k))
        cp.start()
        sent2.append(cp)
    for k in range(1, NZ):
        n = wrap(z + k, NZ)
        remote(st2.at[n], st2.at[n], t2s.at[0], t2r.at[n], up).wait_recv()
    best, mass, moment = merge(st2, 8)
    ent[c] = jnp.broadcast_to(jnp.log(mass) - moment / mass, (8, 256))
    final = remote(ent.at[c], ent.at[c], es_sem.at[0], es_sem.at[1], me.off(dc=1))
    final.start()
    remote(ent.at[1 - c], ent.at[1 - c], es_sem.at[0], es_sem.at[1], me.off(dc=1)).wait_recv()

    @pl.when(jnp.logical_not(holder))
    def _():
        core_copy.wait_recv()

    @pl.when(holder)
    def _():
        core_copy.wait_send()

    @pl.when(prefill & source)
    def _():
        for k in (1, 3, 2):
            remote(lay, lay, ls_sem.at[k], lr_sem.at[NZ], me.off(dx=k)).wait_send()

    @pl.when(prefill & (z != h))
    def _():
        remote(mine, columns_of(z), ls_sem.at[0], lr_sem.at[z], home).wait_send()

    @pl.when(z == h)
    def _():
        for k in range(1, NZ):
            to = wrap(z + k, NZ)
            remote(hidden_part(to), hpart, hs_sem.at[k], hr_sem, me.at(x, y, to, c)).wait_send()

    @pl.when(decode)
    def _():
        for make in late_decode:
            make().wait_send()

    for make in late:
        make().wait_send()
    for cp in sends + sent + sent2 + [final, swap, w_swap, vocab_swap]:
        cp.wait_send()


def c_slot(zz):
    return lax.rem(zz, 2) * 4 + lax.div(zz, 2)


def drain(*steps):
    live = list(steps)
    while live:
        live = [s for s in live if next(s, "end") != "end"]


def body(hidden, attn_gain, kv_weight, queries, cache_kv, lengths, block_owner, out_weight,
         final_gain, vocab_weight):
    d_model = hidden.shape[2]
    owners = jnp.repeat(block_owner, BLK)[None, :]
    vmem = pl.BlockSpec(memory_space=pltpu.VMEM)
    smem = pl.BlockSpec(memory_space=pltpu.SMEM)
    hbm = pl.BlockSpec(memory_space=pl.ANY)
    dma = pltpu.SemaphoreType.DMA
    lay, ent = pl.pallas_call(
        kernel,
        out_shape=(
            jax.ShapeDtypeStruct((TOK, d_model), BF),
            jax.ShapeDtypeStruct((2, 8, 256), F32),
        ),
        in_specs=[vmem, vmem, vmem, smem, vmem, vmem, hbm, hbm, hbm, hbm],
        out_specs=(vmem, vmem),
        scratch_shapes=[
            pltpu.VMEM(kv_weight.shape, BF),
            pltpu.VMEM(cache_kv.shape, BF),
            pltpu.VMEM((2,) + out_weight.shape, BF),
            pltpu.VMEM((2,) + vocab_weight.shape, BF),
            pltpu.VMEM((16, TOK, 256), BF),
            pltpu.VMEM((256, 128), F32),
            pltpu.VMEM((256, 128), F32),
            pltpu.VMEM((256, 128), F32),
            pltpu.VMEM((256, 128), F32),
            pltpu.VMEM((NZ, TOK, COLS), BF),
            pltpu.VMEM((4, TOK, COLS), BF),
            pltpu.VMEM((4, TOK, COLS), BF),
            pltpu.VMEM((4, TOK, COLS), BF),
            pltpu.VMEM((3, TOK, COLS), BF),
            pltpu.VMEM((TOK, COLS), F32),
            pltpu.VMEM((TOK, COLS), BF),
            pltpu.VMEM((NZ, 2, NX, 16, 512), BF),
            pltpu.VMEM((NX, 2, NZ, 16, 1024), BF),
            pltpu.VMEM((2, NZ, NX, 16, 512), BF),
            pltpu.VMEM((256, 512), F32),
            pltpu.VMEM((256, 128), F32),
            pltpu.VMEM((16, 8, 256), F32),
            pltpu.VMEM((8, 8, 256), F32),
            pltpu.VMEM((TOK, COLS), BF),
            dma((KV_PARTS + 2,)),
            dma((CACHE_PARTS,)),
            dma((31,)),
            dma((16,)),
            dma((4,)),
            dma((NZ,)),
            dma,
            dma((2, 4)),
            dma((2, 4)),
            dma((2,)),
            dma((3,)),
            dma((3,)),
            dma((3, 4)),
            dma((3, 4)),
            dma((3, 2, 4)),
            dma((3, 2, 4)),
            dma((3, 4)),
            dma((3, 4)),
            dma((5,)),
            dma((NZ + 2,)),
            dma((16,)),
            dma((16,)),
            dma((NZ,)),
            dma((NZ,)),
            dma((2,)),
        ],
        compiler_params=pltpu.CompilerParams(
            collective_id=0, has_side_effects=True, vmem_limit_bytes=56 * 1024 * 1024
        ),
        cost_estimate=pl.CostEstimate(
            flops=4_000_000_000, bytes_accessed=24_000_000, transcendentals=1_000_000
        ),
        name="step",
    )(hidden[0], attn_gain[None, :], queries[0], lengths, owners, final_gain[None, :],
      kv_weight, cache_kv, out_weight, vocab_weight)
    ent = ent[:, 0]
    low = ent[:, 0:128].reshape(2, 2, NX, 16).transpose(2, 0, 1, 3)
    high = ent[:, 128:256].reshape(2, NX, 2, 16).transpose(1, 0, 2, 3)
    entropy = jnp.concatenate([low, high], axis=3).reshape(512)
    return (lay[None], entropy)


def solution(mesh):
    return jax.shard_map(
        body,
        mesh=mesh,
        in_specs=(
            P("section", "row", None),
            P(),
            P(None, "head"),
            P("section", "row", "head"),
            P("row", None, "head"),
            P("row"),
            P(),
            P("head", "row"),
            P(),
            P(None, ("section", "head", "row")),
        ),
        out_specs=(P("section", "row", None), P()),
        check_vma=False,
    )
```

```python
import functools
import math

import jax
import jax.numpy as jnp
from jax import lax
from jax.experimental import pallas as pl
from jax.experimental.pallas import tpu as pltpu
from jax.sharding import PartitionSpec as P

MESH = pl.DeviceIdType.MESH
BF = jnp.bfloat16
F32 = jnp.float32
EPS = 1e-05
NEG = -1e30
BLK = 4
NX, NY, NZ = 4, 4, 8
TOK = 32
COLS = 1024
CACHE_PARTS = 8
KV_PARTS = 4
HALF = 512
PARTS = (("zyx", 256, 640), ("zxy", 640, 1024), ("xyz", 0, 256))


def dot(a, b):
    return jnp.dot(a, b, preferred_element_type=F32)


def dot_t(a, b):
    return lax.dot_general(a, b, (((1,), (1,)), ((), ())), preferred_element_type=F32)


def wrap(value, n):
    return lax.rem(value + n, n)


class Place:
    def __init__(self):
        s, h, r = (lax.axis_index(a) for a in ("section", "head", "row"))
        self.s, self.h, self.r = s, h, r
        self.x, self.c = lax.div(h, 2), lax.rem(h, 2)
        self.z, self.yh = lax.div(r, 2), lax.rem(r, 2)
        self.y = self.yh * 2 + s
        self.decode = s == 1
        self.prefill = s == 0

    def at(self, x, y, z, c):
        return (lax.rem(y, 2), x * 2 + c, z * 2 + lax.div(y, 2))

    def on(self, axis):
        return {"dx": (self.x, NX), "dy": (self.y, NY), "dz": (self.z, NZ)}[axis]

    def off(self, dx=0, dy=0, dz=0, dc=0):
        x = wrap(self.x + dx, NX) if dx else self.x
        y = wrap(self.y + dy, NY) if dy else self.y
        z = wrap(self.z + dz, NZ) if dz else self.z
        c = 1 - self.c if dc else self.c
        return self.at(x, y, z, c)


def remote(src, dst, ssem, rsem, device):
    return pltpu.make_async_remote_copy(
        src_ref=src, dst_ref=dst, send_sem=ssem, recv_sem=rsem,
        device_id=device, device_id_type=MESH,
    )


def unicast(me, axis, block, ssem, rsem, late):
    at, n = me.on(axis)

    def copy(k):
        ref = block(at)
        return remote(ref, ref, ssem.at[k], rsem.at[at], me.off(**{axis: k}))

    order = [k for d in range(n // 2, 0, -1) for k in sorted({d, n - d})]
    for k in order:
        copy(k).start()
        late.append(functools.partial(copy, k))
    yield
    for k in reversed(order):
        source = wrap(at + k, n)
        ref = block(source)
        remote(ref, ref, ssem.at[0], rsem.at[source], me.off(**{axis: 1})).wait_recv()


def ring4(me, axis, half, ssem, rsem, late):
    at, n = me.on(axis)

    def copy(d, k):
        ref = half(at, d if k == 0 else 1 - d) if k < 2 else half(wrap(at - 1 + 2 * d, n), d)
        return remote(ref, ref, ssem.at[d, k], rsem.at[d, k], me.off(**{axis: 1 - 2 * d}))

    def arrived(d, k):
        near = wrap(at - 1 + 2 * d, n)
        ref = half(near, d if k == 0 else 1 - d) if k < 2 else half(wrap(at + 2, n), d)
        return remote(ref, ref, ssem.at[d, k], rsem.at[d, k], me.off(**{axis: 1}))

    for k in range(2):
        for d in range(2):
            copy(d, k).start()
    yield
    for d in range(2):
        arrived(d, 0).wait_recv()
        copy(d, 2).start()
    yield
    for k in (1, 2):
        for d in range(2):
            arrived(d, k).wait_recv()
    for k in range(3):
        for d in range(2):
            late.append(functools.partial(copy, d, k))


def ring8(me, block, half, ssem, rsem, late, seen=None):
    z = me.z

    def copy(d, k):
        origin = wrap(z - k, NZ) if d == 0 else wrap(z + k, NZ)
        ref = block(origin) if k < 3 else half(origin, d)
        return remote(ref, ref, ssem.at[d, k], rsem.at[d, k], me.off(dz=1 - 2 * d))

    def arrived(d, k):
        origin = wrap(z - 1 - k, NZ) if d == 0 else wrap(z + 1 + k, NZ)
        ref = block(origin) if k < 3 else half(origin, d)
        return remote(ref, ref, ssem.at[d, k], rsem.at[d, k], me.off(dz=1))

    copy(0, 0).start()
    copy(1, 0).start()
    if seen:
        seen(0)
    for k in range(1, 4):
        yield
        for d in range(2):
            arrived(d, k - 1).wait_recv()
            copy(d, k).start()
            if seen:
                seen(k if d else -k)
    yield
    for d in range(2):
        arrived(d, 3).wait_recv()
    if seen:
        seen(4)
    for k in range(4):
        for d in range(2):
            late.append(functools.partial(copy, d, k))


def kernel(
    hid, again, q, lens, block_owner, fgain, kvw_h, cache_h, wout_h, vocab_h,
    lay, ent,
    kvw, cache, wv, vv, kvbuf, qs, m1, l1, o1, abuf, psend, precv, xs, xr, own, hpart, fin,
    b0, b1, b2, acc, ssq, st1, st2, ends,
    lsem, csem, kvs_sem, kvr_sem, vsem, hs_sem, hr_sem, as_sem, ar_sem, ays_sem, ayr_sem,
    ps_sem, xs_sem, xr_sem,
    uni_s, uni_r, p4s, p4r, p8s, p8r, ls_sem, lr_sem, core_sem, t1s, t1r, t2s, t2r, es_sem,
):
    me = Place()
    decode, prefill = me.decode, me.prefill
    x, y, z, c, yh, h, r = me.x, me.y, me.z, me.c, me.yh, me.h, me.r
    d_model = hid.shape[1]
    late = []
    near = wrap(jnp.where(decode, y + 1, y - 1), NY)
    home_y = jnp.where(decode, near, y)
    holder = c == lax.rem(z, 2)
    xz = lax.div(z, 2)

    cache_copies = [
        pltpu.make_async_copy(
            cache_h.at[pl.ds(i * 4, 4)], cache.at[pl.ds(i * 4, 4)], csem.at[i]
        )
        for i in range(CACHE_PARTS)
    ]
    step = d_model // KV_PARTS
    kv_copies = [
        pltpu.make_async_copy(
            kvw_h.at[pl.ds(i * step, step)], kvw.at[pl.ds(i * step, step)], lsem.at[i]
        )
        for i in range(KV_PARTS)
    ]
    w_copy = pltpu.make_async_copy(wout_h, wv, lsem.at[KV_PARTS])
    v_copy = pltpu.make_async_copy(vocab_h, vv.at[0], lsem.at[KV_PARTS + 1])
    for cp in kv_copies:
        cp.start()

    @pl.when(decode)
    def _():
        for cp in cache_copies:
            cp.start()

    w_copy.start()
    v_copy.start()

    peers = [dict(dz=k) for k in range(1, NZ)]
    peers += [dict(dy=2, dz=k) for k in range(1, NZ)]
    peers += [dict(dx=i, dy=j) for i in range(NX) for j in range(NY) if i or j]
    peers += [dict(dc=1)]
    barrier = pltpu.get_barrier_semaphore()
    for p in peers:
        pl.semaphore_signal(barrier, 1, device_id=me.off(**p), device_id_type=MESH)
    for k in range(1, NZ):
        to = me.at(x, near, wrap(z + k, NZ), c)
        pl.semaphore_signal(barrier, 1, device_id=to, device_id_type=MESH)

    @pl.when(prefill & holder)
    def _():
        for k in range(NZ):
            zz = wrap(z + k, NZ)
            pl.semaphore_signal(barrier, 1, device_id=me.at(xz, near, zz, c), device_id_type=MESH)
            if k:
                pl.semaphore_signal(barrier, 1, device_id=me.at(xz, y, zz, c), device_id_type=MESH)

        @pl.when(x != xz)
        def _():
            pl.semaphore_signal(barrier, 1, device_id=me.at(xz, y, z, c), device_id_type=MESH)

    def square(i, total):
        w = hid[:, pl.ds(pl.multiple_of(i * 1024, 1024), 1024)].astype(F32)
        return total + jnp.sum(w * w, axis=1, keepdims=True)

    total = lax.fori_loop(0, d_model // 1024, square, jnp.zeros((TOK, 1), F32))
    inv = lax.rsqrt(total / d_model + EPS)
    fresh = jnp.zeros((TOK, 256), F32)
    for i in range(KV_PARTS):
        kv_copies[i].wait()

        def part(j, sum_, i=i):
            at = pl.ds(pl.multiple_of(i * step + j * 512, 512), 512)
            n = (hid[:, at].astype(F32) * inv * again[:, at]).astype(BF)
            return sum_ + dot(n, kvw[at, :])

        fresh = lax.fori_loop(0, step // 512, part, fresh)
    fresh = fresh.astype(BF)

    for g in range(8):
        qs[pl.ds(g, TOK, stride=8), :] = q[:, g * 128:(g + 1) * 128].astype(F32)
    scale = 1.0 / math.sqrt(128)

    at_home = prefill & (z == h)
    extra = jnp.where(at_home, 3, 4)
    pl.semaphore_wait(barrier, len(peers) + NZ - 1 + extra)

    vocab_swap = remote(vocab_h, vv.at[1], vsem.at[0], vsem.at[1], me.off(dc=1))

    def hidden_part(zz, half):
        return pl.ds(pl.multiple_of(zz * COLS + half * HALF, HALF), HALF)

    def hidden_copy(k, other):
        zz = wrap(z + k, NZ)
        src = hid.at[:, hidden_part(zz, 1 - yh if other else yh)]
        to = me.at(x, near if other else y, zz, c)
        return remote(src, hpart.at[other], hs_sem.at[k, other], hr_sem.at[other], to)

    def send_later_needs():
        vocab_swap.start()

        @pl.when(z == h)
        def _():
            for k in range(NZ):
                if k:
                    hidden_copy(k, 0).start()
                hidden_copy(k, 1).start()
            hpart[0] = hid[:, hidden_part(z, yh)]

    up, down = me.off(dy=1), me.off(dy=-1)

    @pl.when(prefill)
    def _():
        m1[...] = jnp.full_like(m1, NEG)
        l1[...] = jnp.zeros_like(l1)
        o1[...] = jnp.zeros_like(o1)
        kvbuf[r] = fresh
        sent = []
        order = [(0, 1)] + [(k, j) for k in (1, 7, 2, 6, 3, 5, 4) for j in (0, 1)]
        for n, (k, j) in enumerate(order):
            cp = remote(kvbuf.at[r], kvbuf.at[r], kvs_sem.at[n], kvr_sem.at[r],
                        me.off(dz=k, dy=2 * j))
            cp.start()
            sent.append(cp)
        n = 15
        for k in (0, 1, 7, 2, 6, 3, 5, 4):
            i = wrap(z + k, NZ) * 2 + yh
            ref, sem = kvbuf.at[i], kvr_sem.at[i]
            if k:
                remote(ref, ref, kvs_sem.at[n], sem, up).wait_recv()
            for to in (up, down):
                cp = remote(ref, ref, kvs_sem.at[n], sem, to)
                cp.start()
                sent.append(cp)
                n += 1
        send_later_needs()
        for k in range(NZ):
            i = wrap(z + k, NZ) * 2 + 1 - yh
            remote(kvbuf.at[i], kvbuf.at[i], kvs_sem.at[0], kvr_sem.at[i], up).wait_recv()
        for cp in sent:
            cp.wait_send()

    @pl.when(decode)
    def _():
        send_later_needs()
        cache_len = cache.shape[1]

        def rows(first):
            parts = []
            for j in range(4):
                i = first + j
                qi = qs[pl.ds(pl.multiple_of(i * 8, 8), 8), :].astype(BF)
                s = dot_t(qi, cache[i, :, 0:128]) * scale
                at = lax.broadcasted_iota(jnp.int32, (8, cache_len), 1)
                parts.append(jnp.where(at < lens[i], s, NEG))
            s = jnp.concatenate(parts, axis=0)
            top = jnp.max(s, axis=1, keepdims=True)
            p = jnp.exp(s - top)
            total = jnp.sum(p, axis=1, keepdims=True)
            pb = p.astype(BF)
            where = pl.ds(pl.multiple_of(first * 8, 32), 32)
            m1[where, :] = jnp.broadcast_to(top, (32, 128))
            l1[where, :] = jnp.broadcast_to(total, (32, 128))
            out = [dot(pb[8 * j:8 * j + 8], cache[first + j, :, 128:256]) for j in range(4)]
            o1[where, :] = jnp.concatenate(out, axis=0)

        for i in range(CACHE_PARTS):
            cache_copies[i].wait()
            rows(i * 4)
        for i in range(16):
            remote(kvbuf.at[i], kvbuf.at[i], kvs_sem.at[0], kvr_sem.at[i], up).wait_recv()

    keys = kvbuf[:, :, 0:128].reshape(16 * TOK, 128)
    vals = kvbuf[:, :, 128:256].reshape(16 * TOK, 128)
    own_key = fresh[:, 0:128].astype(F32)
    own_val = fresh[:, 128:256].astype(F32)
    flag = jnp.where(decode, 1, 0)
    n_block = block_owner.shape[1]
    digits = jnp.broadcast_to(block_owner[...], (8, n_block))
    spread = lax.broadcasted_iota(jnp.int32, (n_block, n_block * BLK), 1) // BLK
    spread = spread == lax.broadcasted_iota(jnp.int32, (n_block, n_block * BLK), 0)
    spread = spread.astype(F32).astype(BF)
    high = dot((digits >> 4).astype(F32).astype(BF), spread)
    low = dot((digits & 15).astype(F32).astype(BF), spread)
    owners = (high[0:1] * 16.0 + low[0:1]).astype(jnp.int32)

    def a_block(zz, plane):
        return abuf.at[lax.rem(zz, 2), lax.div(zz, 2), plane]

    for half in range(2):
        heads = range(half * 4, half * 4 + 4)
        qh = jnp.concatenate([q[:, g * 128:(g + 1) * 128] for g in heads], axis=0)
        s = dot_t(qh, keys) * scale
        row = r * TOK + lax.rem(lax.broadcasted_iota(jnp.int32, s.shape, 0), TOK)
        tok = lax.broadcasted_iota(jnp.int32, s.shape, 1)
        off = flag * jnp.abs(owners - row) + (1 - flag) * jnp.maximum(tok - row, 0)
        s = jnp.where(off == 0, s, NEG)
        mc = jnp.concatenate([m1[pl.ds(g, TOK, stride=8), :] for g in heads], axis=0)
        lc = jnp.concatenate([l1[pl.ds(g, TOK, stride=8), :] for g in heads], axis=0)
        oc = jnp.concatenate([o1[pl.ds(g, TOK, stride=8), :] for g in heads], axis=0)
        ok = jnp.concatenate([own_key] * 4, axis=0)
        ov = jnp.concatenate([own_val] * 4, axis=0)
        so = jnp.sum(qh.astype(F32) * ok, axis=1, keepdims=True) * scale
        so = jnp.where(jnp.broadcast_to(flag, so.shape) == 1, so, NEG)
        mc, lc = mc[:, 0:1], lc[:, 0:1]
        top = jnp.maximum(jnp.maximum(jnp.max(s, axis=1, keepdims=True), mc), so)
        p = jnp.exp(s - top)
        fac = jnp.exp(mc - top)
        po = jnp.exp(so - top)
        total = jnp.sum(p, axis=1, keepdims=True) + lc * fac + po
        out = dot(p.astype(BF), vals) + oc * fac + po.astype(BF).astype(F32) * ov
        out = (out / total).astype(BF)
        for j, g in enumerate(heads):
            a_block(z, 0)[:, g * 128:(g + 1) * 128] = out[j * TOK:(j + 1) * TOK]

    def share(k):
        zz = wrap(z + k, NZ)
        to = me.at(x, near, z, c)
        return remote(a_block(zz, 0), a_block(zz, 1), ays_sem.at[k % NZ], ayr_sem.at[zz], to)

    drain(ring8(
        me,
        lambda zz: a_block(zz, 0),
        lambda zz, k: a_block(zz, 0).at[pl.ds(k * 16, 16)],
        as_sem, ar_sem, late, seen=lambda k: share(k).start(),
    ))
    w_copy.wait()
    for k in (0, 1, -1, 2, -2, 3, -3, 4):
        share(k).wait_recv()

    def project(parity):
        return dot(abuf[parity].reshape(8 * TOK, COLS), wv[...]).reshape(NX, 2, TOK, HALF)

    psend[...] = project(1 - c).astype(BF)
    swap = remote(psend, precv, ps_sem.at[0], ps_sem.at[1], me.off(dc=1))
    swap.start()
    total = project(c)
    swap.wait_recv()
    total = total + precv[...].astype(F32)
    xs[...] = total.astype(BF)
    sends = []
    for k in (2, 1, 3):
        to = wrap(x + k, NX)
        cp = remote(xs.at[to], xr.at[k - 1], xs_sem.at[k - 1], xr_sem.at[k - 1], me.at(to, y, z, c))
        cp.start()
        sends.append(cp)
    for i in range(NX):
        @pl.when(x == i)
        def _(i=i):
            own[...] = total[i]

    @pl.when(z != h)
    def _():
        hidden_copy(0, 0).wait_recv()

    hidden_copy(0, 1).wait_recv()
    rows_out = own[...] + hpart[...].astype(F32)
    for cp in sends:
        cp.wait_recv()
    for k in range(3):
        rows_out = rows_out + xr[k].astype(F32)
    fin[...] = rows_out.astype(BF)

    rows_d = fin[1 - me.s]
    strip = jnp.concatenate([rows_d[0:16], rows_d[16:32]], axis=1)
    spot = {"x": x, "y": y, "z": z}
    bufs = (b0, b1, b2)
    for (order, lo, hi), buf in zip(PARTS, bufs):
        buf[tuple(spot[a] for a in reversed(order))] = strip[:, lo:hi]

    def way(p):
        order, lo, hi = PARTS[p]
        buf = bufs[p]
        a1, a2, a3 = order
        i2, i3 = spot[a2], spot[a3]
        n1, n2 = buf.shape[2], buf.shape[1]
        yield from unicast(me, "d" + a1, lambda i: buf.at[i3, i2, i], uni_s.at[p], uni_r.at[p], late)
        yield from ring4(
            me, "d" + a2, lambda i, k: buf.at[i3, i, pl.ds(k * (n1 // 2), n1 // 2)],
            p4s.at[p, 0], p4r.at[p, 0], late)
        if a3 == "z":
            yield from ring8(
                me, lambda i: buf.at[i], lambda i, k: buf.at[i, pl.ds(k * (n2 // 2), n2 // 2)],
                p8s, p8r, late)
        else:
            yield from ring4(
                me, "d" + a3, lambda i, k: buf.at[i, pl.ds(k * (n2 // 2), n2 // 2)],
                p4s.at[p, 1], p4r.at[p, 1], late)

    def owner_cols(zz, half):
        return lay.at[:, pl.ds(pl.multiple_of(zz * COLS + half * HALF, HALF), HALF)]

    def owner_copy(k):
        n = z * 2 + yh
        to = me.at(wrap(x + k, NX), home_y, h, c)
        return remote(fin.at[me.s], owner_cols(z, yh), ls_sem.at[k], lr_sem.at[n], to)

    core_copy = remote(lay, lay, core_sem.at[0], core_sem.at[1], me.off(dc=1))

    def prefill_rows():
        for k in (2, 1, 3):
            owner_copy(k).start()

        @pl.when(jnp.logical_not(at_home))
        def _():
            owner_copy(0).start()

        @pl.when(at_home)
        def _():
            owner_cols(z, yh)[...] = fin[0]

        yield
        yield
        yield

        @pl.when(prefill & holder)
        def _():
            for k in range(NZ):
                zz = wrap(z + k, NZ)
                for half in (yh, 1 - yh):
                    def wait(zz=zz, half=half):
                        ref = owner_cols(zz, half)
                        remote(ref, ref, ls_sem.at[0], lr_sem.at[zz * 2 + half], up).wait_recv()
                    if k == 0 and half is yh:
                        pl.when(x != xz)(wait)
                    else:
                        wait()
            core_copy.start()

    drain(*([way(p) for p in range(len(PARTS))] + [prefill_rows()]))

    def held(i_x, i_y, i_z):
        at = {"x": i_x, "y": i_y, "z": i_z}
        pieces = {}
        for (order, lo, hi), buf in zip(PARTS, bufs):
            pieces[lo] = buf[tuple(at[a] for a in reversed(order))]
        line = jnp.concatenate([pieces[lo] for lo in sorted(pieces)], axis=1)
        return line[:, 0:HALF], line[:, HALF:COLS]

    @pl.when(decode & holder)
    def _():
        for zz in range(NZ):
            for half in range(2):
                i_y = jnp.where(yh == half, 2 * yh + 1, 2 * half)
                low, high = held(xz, i_y, zz)
                at = zz * COLS + half * HALF
                lay[0:16, at:at + HALF] = low
                lay[16:32, at:at + HALF] = high
        core_copy.start()

    v_copy.wait()
    vocab_swap.wait_recv()
    acc[...] = jnp.zeros_like(acc)
    ssq[...] = jnp.zeros_like(ssq)

    def block(zz, carry):
        base = pl.multiple_of(zz * COLS, COLS)
        for half in range(2):
            rows = []
            for i_x in range(NX):
                for plane in range(2):
                    rows += held(i_x, 2 * plane + 1 if half == plane else 2 * half, zz)
            rows = jnp.concatenate(rows, axis=0).astype(F32)
            at = pl.ds(base + half * HALF, HALF)
            sq = rows * rows
            ssq[...] += sq[:, 0:128] + sq[:, 128:256] + sq[:, 256:384] + sq[:, 384:512]
            gained = (rows * fgain[:, at]).astype(BF)
            for k in range(2):
                acc[:, k * 256:(k + 1) * 256] += dot(gained, vv[k, at, :])
        return carry

    lax.fori_loop(0, NZ, block, 0)
    inv = lax.rsqrt(jnp.sum(ssq[...], axis=1, keepdims=True) / d_model + EPS)
    logits = acc[...] * inv
    top = jnp.max(logits, axis=1, keepdims=True)
    shifted = logits - top
    e = jnp.exp(shifted)
    mass = jnp.sum(e, axis=1, keepdims=True)
    moment = jnp.sum(e * shifted, axis=1, keepdims=True)
    lane = lax.broadcasted_iota(jnp.int32, (256, 128), 1)
    packed = jnp.where(lane == 0, top, jnp.where(lane == 1, mass, moment))
    here = x * NY + y
    st1[here] = jnp.transpose(packed)[0:8]

    def merge(ref, n):
        tops = [ref[i, 0:1, :] for i in range(n)]
        best = tops[0]
        for t in tops[1:]:
            best = jnp.maximum(best, t)
        mass = jnp.zeros_like(best)
        moment = jnp.zeros_like(best)
        for i in range(n):
            gap = tops[i] - best
            f = jnp.exp(gap)
            mass = mass + f * ref[i, 1:2, :]
            moment = moment + f * (ref[i, 2:3, :] + gap * ref[i, 1:2, :])
        return best, mass, moment

    sent = []
    for i in range(NX):
        for j in range(NY):
            n = i * NY + j
            if n:
                cp = remote(st1.at[here], st1.at[here], t1s.at[n], t1r.at[here], me.off(dx=i, dy=j))
                cp.start()
                sent.append(cp)
    for i in range(NX):
        for j in range(NY):
            if i or j:
                n = wrap(x + i, NX) * NY + wrap(y + j, NY)
                remote(st1.at[n], st1.at[n], t1s.at[0], t1r.at[n], up).wait_recv()
    best, mass, moment = merge(st1, 16)
    st2[z, 0:1, :] = best
    st2[z, 1:2, :] = mass
    st2[z, 2:3, :] = moment
    sent2 = []
    for k in (4, 3, 5, 2, 6, 1, 7):
        cp = remote(st2.at[z], st2.at[z], t2s.at[k], t2r.at[z], me.off(dz=k))
        cp.start()
        sent2.append(cp)
    for k in range(1, NZ):
        n = wrap(z + k, NZ)
        remote(st2.at[n], st2.at[n], t2s.at[0], t2r.at[n], up).wait_recv()
    best, mass, moment = merge(st2, 8)
    ends[c] = jnp.broadcast_to(jnp.log(mass) - moment / mass, (8, 256))
    final = remote(ends.at[c], ends.at[c], es_sem.at[0], es_sem.at[1], me.off(dc=1))
    final.start()
    remote(ends.at[1 - c], ends.at[1 - c], es_sem.at[0], es_sem.at[1], me.off(dc=1)).wait_recv()
    for i in range(NX):
        ent[i:i + 1, :] = jnp.concatenate(
            [ends[k, 0:1, i * 64:(i + 1) * 64] for k in range(2)], axis=1)

    @pl.when(jnp.logical_not(holder))
    def _():
        core_copy.wait_recv()

    @pl.when(holder)
    def _():
        core_copy.wait_send()

    for k in (1, 2, 3):
        owner_copy(k).wait_send()

    @pl.when(jnp.logical_not(at_home))
    def _():
        owner_copy(0).wait_send()

    @pl.when(z == h)
    def _():
        for k in range(NZ):
            if k:
                hidden_copy(k, 0).wait_send()
            hidden_copy(k, 1).wait_send()

    for k in range(NZ):
        share(k).wait_send()
    for make in late:
        make().wait_send()
    for cp in sends + sent + sent2 + [final, swap, vocab_swap]:
        cp.wait_send()


def drain(*steps):
    live = list(steps)
    while live:
        live = [s for s in live if next(s, "end") != "end"]


def body(hidden, attn_gain, kv_weight, queries, cache_kv, lengths, block_owner, out_weight,
         final_gain, vocab_weight):
    d_model = hidden.shape[2]
    vmem = pl.BlockSpec(memory_space=pltpu.VMEM)
    smem = pl.BlockSpec(memory_space=pltpu.SMEM)
    hbm = pl.BlockSpec(memory_space=pl.ANY)
    dma = pltpu.SemaphoreType.DMA
    size = {"x": NX, "y": NY, "z": NZ}
    spread = [
        pltpu.VMEM(tuple(size[a] for a in reversed(order)) + (16, hi - lo), BF)
        for order, lo, hi in PARTS
    ]
    n = len(PARTS)
    lay, ent = pl.pallas_call(
        kernel,
        out_shape=(
            jax.ShapeDtypeStruct((TOK, d_model), BF),
            jax.ShapeDtypeStruct((NX, 128), F32),
        ),
        in_specs=[vmem, vmem, vmem, smem, vmem, vmem, hbm, hbm, hbm, hbm],
        out_specs=(vmem, vmem),
        scratch_shapes=[
            pltpu.VMEM(kv_weight.shape, BF),
            pltpu.VMEM(cache_kv.shape, BF),
            pltpu.VMEM(out_weight.shape, BF),
            pltpu.VMEM((2,) + vocab_weight.shape, BF),
            pltpu.VMEM((16, TOK, 256), BF),
            pltpu.VMEM((256, 128), F32),
            pltpu.VMEM((256, 128), F32),
            pltpu.VMEM((256, 128), F32),
            pltpu.VMEM((256, 128), F32),
            pltpu.VMEM((2, NX, 2, TOK, COLS), BF),
            pltpu.VMEM((NX, 2, TOK, HALF), BF),
            pltpu.VMEM((NX, 2, TOK, HALF), BF),
            pltpu.VMEM((NX, 2, TOK, HALF), BF),
            pltpu.VMEM((3, 2, TOK, HALF), BF),
            pltpu.VMEM((2, TOK, HALF), F32),
            pltpu.VMEM((2, TOK, HALF), BF),
            pltpu.VMEM((2, TOK, HALF), BF),
            *spread,
            pltpu.VMEM((256, 512), F32),
            pltpu.VMEM((256, 128), F32),
            pltpu.VMEM((16, 8, 256), F32),
            pltpu.VMEM((8, 8, 256), F32),
            pltpu.VMEM((2, 8, 256), F32),
            dma((KV_PARTS + 2,)),
            dma((CACHE_PARTS,)),
            dma((31,)),
            dma((16,)),
            dma((2,)),
            dma((NZ, 2)),
            dma((2,)),
            dma((2, 4)),
            dma((2, 4)),
            dma((NZ,)),
            dma((NZ,)),
            dma((2,)),
            dma((3,)),
            dma((3,)),
            dma((n, NZ)),
            dma((n, NZ)),
            dma((n, 2, 2, 3)),
            dma((n, 2, 2, 3)),
            dma((2, 4)),
            dma((2, 4)),
            dma((4,)),
            dma((16,)),
            dma((2,)),
            dma((16,)),
            dma((16,)),
            dma((NZ,)),
            dma((NZ,)),
            dma((2,)),
        ],
        compiler_params=pltpu.CompilerParams(
            collective_id=0, has_side_effects=True, vmem_limit_bytes=56 * 1024 * 1024
        ),
        cost_estimate=pl.CostEstimate(
            flops=4_000_000_000, bytes_accessed=24_000_000, transcendentals=1_000_000
        ),
        name="step",
    )(hidden[0], attn_gain[None, :], queries[0], lengths, block_owner[None, :], final_gain[None, :],
      kv_weight, cache_kv, out_weight, vocab_weight)
    return (lay[None], ent.reshape(512))


def solution(mesh):
    return jax.shard_map(
        body,
        mesh=mesh,
        in_specs=(
            P("section", "row", None),
            P(),
            P(None, "head"),
            P("section", "row", "head"),
            P("row", None, "head"),
            P("row"),
            P(),
            P("head", "row"),
            P(),
            P(None, ("section", "head", "row")),
        ),
        out_specs=(P("section", "row", None), P()),
        check_vma=False,
    )
```

```python
import functools
import math

import jax
import jax.numpy as jnp
from jax import lax
from jax.experimental import pallas as pl
from jax.experimental.pallas import tpu as pltpu
from jax.sharding import PartitionSpec as P

MESH = pl.DeviceIdType.MESH
BF = jnp.bfloat16
F32 = jnp.float32
EPS = 1e-05
NEG = -1e30
BLK = 4
NX, NY, NZ = 4, 4, 8
TOK = 32
COLS = 1024
CACHE_PARTS = 8
KV_PARTS = 4
HALF = 512
PARTS = (("xyz", 0, 256), ("zyx", 256, 640), ("zxy", 640, 1024))


def dot(a, b):
    return jnp.dot(a, b, preferred_element_type=F32)


def dot_t(a, b):
    return lax.dot_general(a, b, (((1,), (1,)), ((), ())), preferred_element_type=F32)


def wrap(value, n):
    return lax.rem(value + n, n)


class Place:
    def __init__(self):
        s, h, r = (lax.axis_index(a) for a in ("section", "head", "row"))
        self.s, self.h, self.r = s, h, r
        self.x, self.c = lax.div(h, 2), lax.rem(h, 2)
        self.z, self.yh = lax.div(r, 2), lax.rem(r, 2)
        self.y = self.yh * 2 + s
        self.decode = s == 1
        self.prefill = s == 0

    def at(self, x, y, z, c):
        return (lax.rem(y, 2), x * 2 + c, z * 2 + lax.div(y, 2))

    def on(self, axis):
        return {"dx": (self.x, NX), "dy": (self.y, NY), "dz": (self.z, NZ)}[axis]

    def off(self, dx=0, dy=0, dz=0, dc=0):
        x = wrap(self.x + dx, NX) if dx else self.x
        y = wrap(self.y + dy, NY) if dy else self.y
        z = wrap(self.z + dz, NZ) if dz else self.z
        c = 1 - self.c if dc else self.c
        return self.at(x, y, z, c)


def remote(src, dst, ssem, rsem, device):
    return pltpu.make_async_remote_copy(
        src_ref=src, dst_ref=dst, send_sem=ssem, recv_sem=rsem,
        device_id=device, device_id_type=MESH,
    )


def unicast(me, axis, block, ssem, rsem, late):
    at, n = me.on(axis)

    def copy(k):
        ref = block(at)
        return remote(ref, ref, ssem.at[k], rsem.at[at], me.off(**{axis: k}))

    order = [k for d in range(n // 2, 0, -1) for k in sorted({d, n - d})]
    for k in order:
        copy(k).start()
        late.append(functools.partial(copy, k))
    yield
    for k in reversed(order):
        source = wrap(at + k, n)
        ref = block(source)
        remote(ref, ref, ssem.at[0], rsem.at[source], me.off(**{axis: 1})).wait_recv()


def ring4(me, axis, half, ssem, rsem, late):
    at, n = me.on(axis)

    def copy(d, k):
        ref = half(at, d if k == 0 else 1 - d) if k < 2 else half(wrap(at - 1 + 2 * d, n), d)
        return remote(ref, ref, ssem.at[d, k], rsem.at[d, k], me.off(**{axis: 1 - 2 * d}))

    def arrived(d, k):
        near = wrap(at - 1 + 2 * d, n)
        ref = half(near, d if k == 0 else 1 - d) if k < 2 else half(wrap(at + 2, n), d)
        return remote(ref, ref, ssem.at[d, k], rsem.at[d, k], me.off(**{axis: 1}))

    for k in range(2):
        for d in range(2):
            copy(d, k).start()
    yield
    for d in range(2):
        arrived(d, 0).wait_recv()
        copy(d, 2).start()
    yield "tail"
    for k in (1, 2):
        for d in range(2):
            arrived(d, k).wait_recv()
    for k in range(3):
        for d in range(2):
            late.append(functools.partial(copy, d, k))


def ring8(me, block, half, ssem, rsem, late, seen=None):
    z = me.z

    def copy(d, k):
        origin = wrap(z - k, NZ) if d == 0 else wrap(z + k, NZ)
        ref = block(origin) if k < 3 else half(origin, d)
        return remote(ref, ref, ssem.at[d, k], rsem.at[d, k], me.off(dz=1 - 2 * d))

    def arrived(d, k):
        origin = wrap(z - 1 - k, NZ) if d == 0 else wrap(z + 1 + k, NZ)
        ref = block(origin) if k < 3 else half(origin, d)
        return remote(ref, ref, ssem.at[d, k], rsem.at[d, k], me.off(dz=1))

    copy(0, 0).start()
    copy(1, 0).start()
    if seen:
        seen(0)
    for k in range(1, 4):
        yield
        for d in range(2):
            arrived(d, k - 1).wait_recv()
            copy(d, k).start()
            if seen:
                seen(k if d else -k)
    yield "tail"
    for d in range(2):
        arrived(d, 3).wait_recv()
    if seen:
        seen(4)
    for k in range(4):
        for d in range(2):
            late.append(functools.partial(copy, d, k))


def kernel(
    hid, again, q, lens, block_owner, fgain, kvw_h, cache_h, wout_h, vocab_h,
    lay_out, ent,
    lay, kvw, cache, wv, vv, kvbuf, qs, m1, l1, o1, abuf, psend, precv, xs, xr, own, hpart, fin,
    *rest,
):
    bufs = rest[:len(PARTS)]
    (
        acc, ssq, st1, st2,
        lsem, csem, kvs_sem, kvr_sem, vsem, hs_sem, hr_sem, as_sem, ar_sem, ays_sem, ayr_sem, fs_sem, fr_sem,
        ps_sem, xs_sem, xr_sem,
        uni_s, uni_r, p4s, p4r, p8s, p8r, ls_sem, lr_sem, core_sem, t1s, t1r, t2s, t2r, es_sem,
    ) = rest[len(PARTS):]
    me = Place()
    decode, prefill = me.decode, me.prefill
    x, y, z, c, yh, h, r = me.x, me.y, me.z, me.c, me.yh, me.h, me.r
    d_model = hid.shape[1]
    late = []
    near = wrap(jnp.where(decode, y + 1, y - 1), NY)
    home_y = jnp.where(decode, near, y)
    holder = c == lax.rem(z, 2)
    xz = lax.div(z, 2)

    cache_copies = [
        pltpu.make_async_copy(
            cache_h.at[pl.ds(i * 4, 4)], cache.at[pl.ds(i * 4, 4)], csem.at[i]
        )
        for i in range(CACHE_PARTS)
    ]
    step = d_model // KV_PARTS
    kv_copies = [
        pltpu.make_async_copy(
            kvw_h.at[pl.ds(i * step, step)], kvw.at[pl.ds(i * step, step)], lsem.at[i]
        )
        for i in range(KV_PARTS)
    ]
    w_copy = pltpu.make_async_copy(wout_h, wv, lsem.at[KV_PARTS])
    v_copy = pltpu.make_async_copy(vocab_h, vv.at[0], lsem.at[KV_PARTS + 1])
    for cp in kv_copies:
        cp.start()

    @pl.when(decode)
    def _():
        for cp in cache_copies:
            cp.start()

    w_copy.start()
    v_copy.start()

    @pl.when(prefill)
    def _():
        kvbuf[...] = jnp.zeros_like(kvbuf)

    peers = [dict(dz=k) for k in range(1, NZ)]
    peers += [dict(dy=2, dz=k) for k in range(1, NZ)]
    peers += [dict(dx=i, dy=j) for i in range(NX) for j in range(NY) if i or j]
    peers += [dict(dc=1, dz=k) for k in range(NZ)]
    barrier = pltpu.get_barrier_semaphore()
    for p in peers:
        pl.semaphore_signal(barrier, 1, device_id=me.off(**p), device_id_type=MESH)
    for k in range(1, NZ):
        to = me.at(x, near, wrap(z + k, NZ), c)
        pl.semaphore_signal(barrier, 1, device_id=to, device_id_type=MESH)

    @pl.when(prefill & holder)
    def _():
        for k in range(NZ):
            zz = wrap(z + k, NZ)
            pl.semaphore_signal(barrier, 1, device_id=me.at(xz, near, zz, c), device_id_type=MESH)
            if k:
                pl.semaphore_signal(barrier, 1, device_id=me.at(xz, y, zz, c), device_id_type=MESH)

        @pl.when(x != xz)
        def _():
            pl.semaphore_signal(barrier, 1, device_id=me.at(xz, y, z, c), device_id_type=MESH)

    def square(i, total):
        w = hid[:, pl.ds(pl.multiple_of(i * 1024, 1024), 1024)].astype(F32)
        return total + jnp.sum(w * w, axis=1, keepdims=True)

    total = lax.fori_loop(0, d_model // 1024, square, jnp.zeros((TOK, 1), F32))
    inv = lax.rsqrt(total / d_model + EPS)
    fresh = jnp.zeros((TOK, 256), F32)
    for i in range(KV_PARTS):
        kv_copies[i].wait()

        def part(j, sum_, i=i):
            at = pl.ds(pl.multiple_of(i * step + j * 512, 512), 512)
            n = (hid[:, at].astype(F32) * inv * again[:, at]).astype(BF)
            return sum_ + dot(n, kvw[at, :])

        fresh = lax.fori_loop(0, step // 512, part, fresh)
    fresh = fresh.astype(BF)

    for g in range(8):
        qs[pl.ds(g, TOK, stride=8), :] = q[:, g * 128:(g + 1) * 128].astype(F32)
    scale = 1.0 / math.sqrt(128)

    at_home = prefill & (z == h)
    extra = jnp.where(at_home, 3, 4)
    pl.semaphore_wait(barrier, len(peers) + NZ - 1 + extra)

    vocab_swap = remote(vocab_h, vv.at[1], vsem.at[0], vsem.at[1], me.off(dc=1))

    def hidden_part(zz, half):
        return pl.ds(pl.multiple_of(zz * COLS + half * HALF, HALF), HALF)

    def hidden_copy(k, other):
        zz = wrap(z + k, NZ)
        src = hid.at[:, hidden_part(zz, 1 - yh if other else yh)]
        to = me.at(x, near if other else y, zz, c)
        return remote(src, hpart.at[other], hs_sem.at[k, other], hr_sem.at[other], to)

    def send_later_needs():
        vocab_swap.start()

        @pl.when(z == h)
        def _():
            for k in range(NZ):
                if k:
                    hidden_copy(k, 0).start()
                hidden_copy(k, 1).start()
            hpart[0] = hid[:, hidden_part(z, yh)]

    up, down = me.off(dy=1), me.off(dy=-1)

    @pl.when(prefill)
    def _():
        m1[...] = jnp.full_like(m1, NEG)
        l1[...] = jnp.zeros_like(l1)
        o1[...] = jnp.zeros_like(o1)
        kvbuf[r] = fresh
        sent = []
        for n, k in enumerate((1, 7, 2, 6, 3, 5, 4)):
            cp = remote(kvbuf.at[r], kvbuf.at[r], kvs_sem.at[n], kvr_sem.at[r], me.off(dz=k))
            cp.start()
            sent.append(cp)

        def across(k):
            return remote(kvbuf.at[r], kvbuf.at[r], kvs_sem.at[23 + k], kvr_sem.at[r],
                          me.off(dz=k, dy=2))

        across(0).start()
        for k in range(1, NZ):
            @pl.when(z + k < NZ)
            def _(k=k):
                across(k).start()

        n = 7
        for k in (0, 1, 7, 2, 6, 3, 5, 4):
            i = wrap(z + k, NZ) * 2 + yh
            ref, sem = kvbuf.at[i], kvr_sem.at[i]
            if k:
                remote(ref, ref, kvs_sem.at[n], sem, up).wait_recv()
            for to in (up, down):
                cp = remote(ref, ref, kvs_sem.at[n], sem, to)
                cp.start()
                sent.append(cp)
                n += 1
        send_later_needs()
        for k in range(NZ):
            @pl.when(k <= z)
            def _(k=k):
                i = k * 2 + 1 - yh
                remote(kvbuf.at[i], kvbuf.at[i], kvs_sem.at[0], kvr_sem.at[i], up).wait_recv()

        for cp in sent:
            cp.wait_send()
        across(0).wait_send()
        for k in range(1, NZ):
            @pl.when(z + k < NZ)
            def _(k=k):
                across(k).wait_send()

    @pl.when(decode)
    def _():
        send_later_needs()
        cache_len = cache.shape[1]

        def rows(first):
            parts = []
            for j in range(4):
                i = first + j
                qi = qs[pl.ds(pl.multiple_of(i * 8, 8), 8), :].astype(BF)
                s = dot_t(qi, cache[i, :, 0:128]) * scale
                at = lax.broadcasted_iota(jnp.int32, (8, cache_len), 1)
                parts.append(jnp.where(at < lens[i], s, NEG))
            s = jnp.concatenate(parts, axis=0)
            top = jnp.max(s, axis=1, keepdims=True)
            p = jnp.exp(s - top)
            total = jnp.sum(p, axis=1, keepdims=True)
            pb = p.astype(BF)
            where = pl.ds(pl.multiple_of(first * 8, 32), 32)
            m1[where, :] = jnp.broadcast_to(top, (32, 128))
            l1[where, :] = jnp.broadcast_to(total, (32, 128))
            out = [dot(pb[8 * j:8 * j + 8], cache[first + j, :, 128:256]) for j in range(4)]
            o1[where, :] = jnp.concatenate(out, axis=0)

        for i in range(CACHE_PARTS):
            cache_copies[i].wait()
            rows(i * 4)
        for i in range(16):
            remote(kvbuf.at[i], kvbuf.at[i], kvs_sem.at[0], kvr_sem.at[i], up).wait_recv()

    keys = kvbuf[:, :, 0:128].reshape(16 * TOK, 128)
    vals = kvbuf[:, :, 128:256].reshape(16 * TOK, 128)
    own_key = fresh[:, 0:128].astype(F32)
    own_val = fresh[:, 128:256].astype(F32)
    flag = jnp.where(decode, 1, 0)
    n_block = block_owner.shape[1]
    digits = jnp.broadcast_to(block_owner[...], (8, n_block))
    spread = lax.broadcasted_iota(jnp.int32, (n_block, n_block * BLK), 1) // BLK
    spread = spread == lax.broadcasted_iota(jnp.int32, (n_block, n_block * BLK), 0)
    spread = spread.astype(F32).astype(BF)
    high = dot((digits >> 4).astype(F32).astype(BF), spread)
    low = dot((digits & 15).astype(F32).astype(BF), spread)
    owners = (high[0:1] * 16.0 + low[0:1]).astype(jnp.int32)

    def a_block(zz, plane, part):
        return abuf.at[lax.rem(zz, 2), part, lax.div(zz, 2), plane]

    def share(k, part):
        zz = wrap(z + k, NZ)
        to = me.at(x, near, z, c)
        return remote(a_block(zz, 0, part), a_block(zz, 1, part),
                      ays_sem.at[part, k % NZ], ayr_sem.at[part, zz], to)

    def share_far(d, part):
        zz = wrap(z - 3 + 6 * d, NZ)
        to = me.at(x, near, wrap(z + 1 - 2 * d, NZ), c)
        rows = pl.ds(d * 16, 16)
        return remote(a_block(zz, 0, part).at[rows], a_block(zz, 1, part).at[rows],
                      fs_sem.at[part, d], fr_sem.at[part, d], to)

    def shared_far(d, part):
        zz = wrap(z + 4, NZ)
        rows = pl.ds(d * 16, 16)
        return remote(a_block(zz, 0, part).at[rows], a_block(zz, 1, part).at[rows],
                      fs_sem.at[part, d], fr_sem.at[part, d], me.at(x, near, z, c))

    def a_ring(part):
        def seen(k):
            if k == 4:
                return
            if abs(k) == 3:
                share_far(0 if k < 0 else 1, part).start()
            share(k, part).start()

        return ring8(
            me,
            lambda zz: a_block(zz, 0, part),
            lambda zz, k: a_block(zz, 0, part).at[pl.ds(k * 16, 16)],
            as_sem.at[part], ar_sem.at[part], late, seen=seen,
        )

    rings = []

    for half in range(2):
        heads = range(half * 4, half * 4 + 4)
        qh = jnp.concatenate([q[:, g * 128:(g + 1) * 128] for g in heads], axis=0)
        s = dot_t(qh, keys) * scale
        row = r * TOK + lax.rem(lax.broadcasted_iota(jnp.int32, s.shape, 0), TOK)
        tok = lax.broadcasted_iota(jnp.int32, s.shape, 1)
        off = flag * jnp.abs(owners - row) + (1 - flag) * jnp.maximum(tok - row, 0)
        s = jnp.where(off == 0, s, NEG)
        mc = jnp.concatenate([m1[pl.ds(g, TOK, stride=8), :] for g in heads], axis=0)
        lc = jnp.concatenate([l1[pl.ds(g, TOK, stride=8), :] for g in heads], axis=0)
        oc = jnp.concatenate([o1[pl.ds(g, TOK, stride=8), :] for g in heads], axis=0)
        ok = jnp.concatenate([own_key] * 4, axis=0)
        ov = jnp.concatenate([own_val] * 4, axis=0)
        so = jnp.sum(qh.astype(F32) * ok, axis=1, keepdims=True) * scale
        so = jnp.where(jnp.broadcast_to(flag, so.shape) == 1, so, NEG)
        mc, lc = mc[:, 0:1], lc[:, 0:1]
        top = jnp.maximum(jnp.maximum(jnp.max(s, axis=1, keepdims=True), mc), so)
        p = jnp.exp(s - top)
        fac = jnp.exp(mc - top)
        po = jnp.exp(so - top)
        total = jnp.sum(p, axis=1, keepdims=True) + lc * fac + po
        out = dot(p.astype(BF), vals) + oc * fac + po.astype(BF).astype(F32) * ov
        out = (out / total).astype(BF)
        for j, g in enumerate(heads):
            a_block(z, 0, half)[:, j * 128:(j + 1) * 128] = out[j * TOK:(j + 1) * TOK]
        rings.append(a_ring(half))
        next(rings[-1])

    drain(*rings)
    w_copy.wait()
    for part in range(2):
        for k in (0, 1, -1, 2, -2, 3, -3):
            share(k, part).wait_recv()
        for d in range(2):
            shared_far(d, part).wait_recv()

    def project(parity):
        rows = [abuf[parity, part].reshape(8 * TOK, HALF) for part in range(2)]
        total = dot(rows[0], wv[0:HALF, :]) + dot(rows[1], wv[HALF:COLS, :])
        return total.reshape(NX, 2, TOK, HALF)

    psend[...] = project(1 - c).astype(BF)
    swap = remote(psend, precv, ps_sem.at[0], ps_sem.at[1], me.off(dc=1))
    swap.start()
    total = project(c)
    swap.wait_recv()
    total = total + precv[...].astype(F32)
    xs[...] = total.astype(BF)
    sends = []
    for k in (2, 1, 3):
        to = wrap(x + k, NX)
        cp = remote(xs.at[to], xr.at[k - 1], xs_sem.at[k - 1], xr_sem.at[k - 1], me.at(to, y, z, c))
        cp.start()
        sends.append(cp)
    for i in range(NX):
        @pl.when(x == i)
        def _(i=i):
            own[...] = total[i]

    @pl.when(z != h)
    def _():
        hidden_copy(0, 0).wait_recv()

    hidden_copy(0, 1).wait_recv()
    rows_out = own[...] + hpart[...].astype(F32)
    for cp in sends:
        cp.wait_recv()
    for k in range(3):
        rows_out = rows_out + xr[k].astype(F32)
    fin[...] = rows_out.astype(BF)

    rows_d = fin[1 - me.s]
    strip = jnp.concatenate([rows_d[0:16], rows_d[16:32]], axis=1)
    spot = {"x": x, "y": y, "z": z}
    for (order, lo, hi), buf in zip(PARTS, bufs):
        buf[tuple(spot[a] for a in reversed(order))] = strip[:, lo:hi]

    def way(p):
        order, lo, hi = PARTS[p]
        buf = bufs[p]
        a1, a2, a3 = order
        i2, i3 = spot[a2], spot[a3]
        n1, n2 = buf.shape[2], buf.shape[1]
        yield from unicast(me, "d" + a1, lambda i: buf.at[i3, i2, i], uni_s.at[p], uni_r.at[p], late)
        if a2 == "z":
            yield from ring8(
                me, lambda i: buf.at[i3, i],
                lambda i, k: buf.at[i3, i, pl.ds(k * (n1 // 2), n1 // 2)], p8s.at[p], p8r.at[p], late)
        else:
            yield from ring4(
                me, "d" + a2, lambda i, k: buf.at[i3, i, pl.ds(k * (n1 // 2), n1 // 2)],
                p4s.at[p, 0], p4r.at[p, 0], late)
        if a3 == "z":
            yield from last(ring8(
                me, lambda i: buf.at[i], lambda i, k: buf.at[i, pl.ds(k * (n2 // 2), n2 // 2)],
                p8s.at[p], p8r.at[p], late))
        else:
            yield from last(ring4(
                me, "d" + a3, lambda i, k: buf.at[i, pl.ds(k * (n2 // 2), n2 // 2)],
                p4s.at[p, 1], p4r.at[p, 1], late))

    def owner_cols(zz, half):
        return lay.at[:, pl.ds(pl.multiple_of(zz * COLS + half * HALF, HALF), HALF)]

    def owner_copy(k):
        n = z * 2 + yh
        to = me.at(wrap(x + k, NX), home_y, h, c)
        return remote(fin.at[me.s], owner_cols(z, yh), ls_sem.at[k], lr_sem.at[n], to)

    core_copy = remote(lay, lay, core_sem.at[0], core_sem.at[1], me.off(dc=1))

    drain(*[way(p) for p in range(len(PARTS))])

    for k in (2, 1, 3):
        owner_copy(k).start()

    @pl.when(jnp.logical_not(at_home))
    def _():
        owner_copy(0).start()

    @pl.when(at_home)
    def _():
        owner_cols(z, yh)[...] = fin[0]

    def held(i_x, i_y, i_z):
        at = {"x": i_x, "y": i_y, "z": i_z}
        pieces = {}
        for (order, lo, hi), buf in zip(PARTS, bufs):
            pieces[lo] = buf[tuple(at[a] for a in reversed(order))]
        line = jnp.concatenate([pieces[lo] for lo in sorted(pieces)], axis=1)
        return line[:, 0:HALF], line[:, HALF:COLS]

    @pl.when(decode & holder)
    def _():
        for zz in range(NZ):
            for half in range(2):
                i_y = jnp.where(yh == half, 2 * yh + 1, 2 * half)
                low, high = held(xz, i_y, zz)
                at = zz * COLS + half * HALF
                lay[0:16, at:at + HALF] = low
                lay[16:32, at:at + HALF] = high
        core_copy.start()

    v_copy.wait()
    vocab_swap.wait_recv()
    acc[...] = jnp.zeros_like(acc)
    ssq[...] = jnp.zeros_like(ssq)

    def block(zz, carry):
        base = pl.multiple_of(zz * COLS, COLS)
        for half in range(2):
            rows = []
            for i_x in range(NX):
                for plane in range(2):
                    rows += held(i_x, 2 * plane + 1 if half == plane else 2 * half, zz)
            rows = jnp.concatenate(rows, axis=0).astype(F32)
            at = pl.ds(base + half * HALF, HALF)
            sq = rows * rows
            ssq[...] += sq[:, 0:128] + sq[:, 128:256] + sq[:, 256:384] + sq[:, 384:512]
            gained = (rows * fgain[:, at]).astype(BF)
            for k in range(2):
                acc[:, k * 256:(k + 1) * 256] += dot(gained, vv[k, at, :])
        return carry

    lax.fori_loop(0, NZ, block, 0)
    inv = lax.rsqrt(jnp.sum(ssq[...], axis=1, keepdims=True) / d_model + EPS)
    logits = acc[...] * inv
    top = jnp.max(logits, axis=1, keepdims=True)
    shifted = logits - top
    e = jnp.exp(shifted)
    mass = jnp.sum(e, axis=1, keepdims=True)
    moment = jnp.sum(e * shifted, axis=1, keepdims=True)
    lane = lax.broadcasted_iota(jnp.int32, (256, 128), 1)
    packed = jnp.where(lane == 0, top, jnp.where(lane == 1, mass, moment))
    here = x * NY + y
    lines = jnp.transpose(packed)
    st1[here] = jnp.concatenate(
        [lines[i:i + 1, j * 128:(j + 1) * 128] for i in (0, 1, 2, 2) for j in range(2)], axis=0)

    def merge(ref, n):
        tops = [ref[i, 0:2, :] for i in range(n)]
        best = tops[0]
        for t in tops[1:]:
            best = jnp.maximum(best, t)
        mass = jnp.zeros_like(best)
        moment = jnp.zeros_like(best)
        for i in range(n):
            gap = tops[i] - best
            f = jnp.exp(gap)
            mass = mass + f * ref[i, 2:4, :]
            moment = moment + f * (ref[i, 4:6, :] + gap * ref[i, 2:4, :])
        return best, mass, moment

    sent = []
    for i in range(NX):
        for j in range(NY):
            n = i * NY + j
            if n:
                cp = remote(st1.at[here], st1.at[here], t1s.at[n], t1r.at[here], me.off(dx=i, dy=j))
                cp.start()
                sent.append(cp)
    for i in range(NX):
        for j in range(NY):
            if i or j:
                n = wrap(x + i, NX) * NY + wrap(y + j, NY)
                remote(st1.at[n], st1.at[n], t1s.at[0], t1r.at[n], up).wait_recv()
    best, mass, moment = merge(st1, 16)
    st2[c, z] = jnp.concatenate([best, mass, moment, moment], axis=0)

    def totals(k, other):
        return remote(st2.at[c, z], st2.at[c, z], t2s.at[k, other], t2r.at[c, z],
                      me.off(dz=k, dc=other))

    last_step = [(k, j) for k in (4, 3, 5, 2, 6, 1, 7, 0) for j in (0, 1) if k or j]
    for k, j in last_step:
        totals(k, j).start()

    @pl.when(prefill & holder)
    def _():
        for k in range(NZ):
            zz = wrap(z + k, NZ)
            for half in (yh, 1 - yh):
                def wait(zz=zz, half=half):
                    ref = owner_cols(zz, half)
                    remote(ref, ref, ls_sem.at[0], lr_sem.at[zz * 2 + half], up).wait_recv()
                if k == 0 and half is yh:
                    pl.when(x != xz)(wait)
                else:
                    wait()
        core_copy.start()

    @pl.when(jnp.logical_not(holder))
    def _():
        core_copy.wait_recv()

    out_copy = pltpu.make_async_copy(lay, lay_out, es_sem)
    out_copy.start()
    for i in range(NZ):
        for j in range(2):
            at = 1 - c if j else c
            n = wrap(z + i, NZ)
            if i or j:
                remote(st2.at[at, n], st2.at[at, n], t2s.at[0, 0], t2r.at[at, n], up).wait_recv()
    sides = []
    for j in range(2):
        best, mass, moment = merge(st2.at[j], NZ)
        sides.append(jnp.log(mass) - moment / mass)
    for i in range(NX):
        at = (i % 2) * 64
        ent[i:i + 1, :] = jnp.concatenate(
            [side[i // 2:i // 2 + 1, at:at + 64] for side in sides], axis=1)
    out_copy.wait()

    @pl.when(holder)
    def _():
        core_copy.wait_send()

    for k in (1, 2, 3):
        owner_copy(k).wait_send()

    @pl.when(jnp.logical_not(at_home))
    def _():
        owner_copy(0).wait_send()

    @pl.when(z == h)
    def _():
        for k in range(NZ):
            if k:
                hidden_copy(k, 0).wait_send()
            hidden_copy(k, 1).wait_send()

    for part in range(2):
        for k in (0, 1, -1, 2, -2, 3, -3):
            share(k, part).wait_send()
        for d in range(2):
            share_far(d, part).wait_send()
    for make in late:
        make().wait_send()
    for k, j in last_step:
        totals(k, j).wait_send()
    for cp in sends + sent + [swap, vocab_swap]:
        cp.wait_send()


def drain(*steps):
    live, ends = list(steps), []
    while live:
        going = []
        for s in live:
            told = next(s, "end")
            if told == "last":
                ends.append(s)
            elif told != "end":
                going.append(s)
        live = going
    for s in ends:
        for _ in s:
            pass


def last(steps):
    for told in steps:
        yield "last" if told == "tail" else told


def body(hidden, attn_gain, kv_weight, queries, cache_kv, lengths, block_owner, out_weight,
         final_gain, vocab_weight):
    d_model = hidden.shape[2]
    vmem = pl.BlockSpec(memory_space=pltpu.VMEM)
    smem = pl.BlockSpec(memory_space=pltpu.SMEM)
    hbm = pl.BlockSpec(memory_space=pl.ANY)
    dma = pltpu.SemaphoreType.DMA
    size = {"x": NX, "y": NY, "z": NZ}
    spread = [
        pltpu.VMEM(tuple(size[a] for a in reversed(order)) + (16, hi - lo), BF)
        for order, lo, hi in PARTS
    ]
    n = len(PARTS)
    lay, ent = pl.pallas_call(
        kernel,
        out_shape=(
            jax.ShapeDtypeStruct((TOK, d_model), BF),
            jax.ShapeDtypeStruct((NX, 128), F32),
        ),
        in_specs=[vmem, vmem, vmem, smem, vmem, vmem, hbm, hbm, hbm, hbm],
        out_specs=(hbm, vmem),
        scratch_shapes=[
            pltpu.VMEM((TOK, d_model), BF),
            pltpu.VMEM(kv_weight.shape, BF),
            pltpu.VMEM(cache_kv.shape, BF),
            pltpu.VMEM(out_weight.shape, BF),
            pltpu.VMEM((2,) + vocab_weight.shape, BF),
            pltpu.VMEM((16, TOK, 256), BF),
            pltpu.VMEM((256, 128), F32),
            pltpu.VMEM((256, 128), F32),
            pltpu.VMEM((256, 128), F32),
            pltpu.VMEM((256, 128), F32),
            pltpu.VMEM((2, 2, NX, 2, TOK, HALF), BF),
            pltpu.VMEM((NX, 2, TOK, HALF), BF),
            pltpu.VMEM((NX, 2, TOK, HALF), BF),
            pltpu.VMEM((NX, 2, TOK, HALF), BF),
            pltpu.VMEM((3, 2, TOK, HALF), BF),
            pltpu.VMEM((2, TOK, HALF), F32),
            pltpu.VMEM((2, TOK, HALF), BF),
            pltpu.VMEM((2, TOK, HALF), BF),
            *spread,
            pltpu.VMEM((256, 512), F32),
            pltpu.VMEM((256, 128), F32),
            pltpu.VMEM((16, 8, 128), F32),
            pltpu.VMEM((2, NZ, 8, 128), F32),
            dma((KV_PARTS + 2,)),
            dma((CACHE_PARTS,)),
            dma((31,)),
            dma((16,)),
            dma((2,)),
            dma((NZ, 2)),
            dma((2,)),
            dma((2, 2, 4)),
            dma((2, 2, 4)),
            dma((2, NZ)),
            dma((2, NZ)),
            dma((2, 2)),
            dma((2, 2)),
            dma((2,)),
            dma((3,)),
            dma((3,)),
            dma((n, NZ)),
            dma((n, NZ)),
            dma((n, 2, 2, 3)),
            dma((n, 2, 2, 3)),
            dma((n, 2, 4)),
            dma((n, 2, 4)),
            dma((4,)),
            dma((16,)),
            dma((2,)),
            dma((16,)),
            dma((16,)),
            dma((NZ, 2)),
            dma((2, NZ)),
            dma,
        ],
        compiler_params=pltpu.CompilerParams(
            collective_id=0, has_side_effects=True, vmem_limit_bytes=56 * 1024 * 1024
        ),
        cost_estimate=pl.CostEstimate(
            flops=4_000_000_000, bytes_accessed=24_000_000, transcendentals=1_000_000
        ),
        name="step",
    )(hidden[0], attn_gain[None, :], queries[0], lengths, block_owner[None, :], final_gain[None, :],
      kv_weight, cache_kv, out_weight, vocab_weight)
    return (lay[None], ent.reshape(512))


def solution(mesh):
    return jax.shard_map(
        body,
        mesh=mesh,
        in_specs=(
            P("section", "row", None),
            P(),
            P(None, "head"),
            P("section", "row", "head"),
            P("row", None, "head"),
            P("row"),
            P(),
            P("head", "row"),
            P(),
            P(None, ("section", "head", "row")),
        ),
        out_specs=(P("section", "row", None), P()),
        check_vma=False,
    )
```

```python
import functools
import math

import jax
import jax.numpy as jnp
from jax import lax
from jax.experimental import pallas as pl
from jax.experimental.pallas import tpu as pltpu
from jax.sharding import PartitionSpec as P

MESH = pl.DeviceIdType.MESH
BF = jnp.bfloat16
F32 = jnp.float32
EPS = 1e-05
NEG = -1e30
BLK = 4
NX, NY, NZ = 4, 4, 8
TOK = 32
COLS = 1024
CACHE_PARTS = 8
KV_PARTS = 4
HALF = 512
PARTS = (("yxz", 0, 384), ("zyx", 384, 768), ("zxy", 768, 1024))


def dot(a, b):
    return jnp.dot(a, b, preferred_element_type=F32)


def dot_t(a, b):
    return lax.dot_general(a, b, (((1,), (1,)), ((), ())), preferred_element_type=F32)


def wrap(value, n):
    return lax.rem(value + n, n)


class Place:
    def __init__(self):
        s, h, r = (lax.axis_index(a) for a in ("section", "head", "row"))
        self.s, self.h, self.r = s, h, r
        self.x, self.c = lax.div(h, 2), lax.rem(h, 2)
        self.z, self.yh = lax.div(r, 2), lax.rem(r, 2)
        self.y = self.yh * 2 + s
        self.decode = s == 1
        self.prefill = s == 0

    def at(self, x, y, z, c):
        return (lax.rem(y, 2), x * 2 + c, z * 2 + lax.div(y, 2))

    def on(self, axis):
        return {"dx": (self.x, NX), "dy": (self.y, NY), "dz": (self.z, NZ)}[axis]

    def off(self, dx=0, dy=0, dz=0, dc=0):
        x = wrap(self.x + dx, NX) if dx else self.x
        y = wrap(self.y + dy, NY) if dy else self.y
        z = wrap(self.z + dz, NZ) if dz else self.z
        c = 1 - self.c if dc else self.c
        return self.at(x, y, z, c)


def remote(src, dst, ssem, rsem, device):
    return pltpu.make_async_remote_copy(
        src_ref=src, dst_ref=dst, send_sem=ssem, recv_sem=rsem,
        device_id=device, device_id_type=MESH,
    )


def unicast(me, axis, block, ssem, rsem, late):
    at, n = me.on(axis)

    def copy(k):
        ref = block(at)
        return remote(ref, ref, ssem.at[k], rsem.at[at], me.off(**{axis: k}))

    order = [k for d in range(n // 2, 0, -1) for k in sorted({d, n - d})]
    for k in order:
        copy(k).start()
        late.append(functools.partial(copy, k))
    yield
    for k in reversed(order):
        source = wrap(at + k, n)
        ref = block(source)
        remote(ref, ref, ssem.at[0], rsem.at[source], me.off(**{axis: 1})).wait_recv()


def ring4(me, axis, half, ssem, rsem, late):
    at, n = me.on(axis)

    def copy(d, k):
        ref = half(at, d if k == 0 else 1 - d) if k < 2 else half(wrap(at - 1 + 2 * d, n), d)
        return remote(ref, ref, ssem.at[d, k], rsem.at[d, k], me.off(**{axis: 1 - 2 * d}))

    def arrived(d, k):
        near = wrap(at - 1 + 2 * d, n)
        ref = half(near, d if k == 0 else 1 - d) if k < 2 else half(wrap(at + 2, n), d)
        return remote(ref, ref, ssem.at[d, k], rsem.at[d, k], me.off(**{axis: 1}))

    for k in range(2):
        for d in range(2):
            copy(d, k).start()
    yield
    for d in range(2):
        arrived(d, 0).wait_recv()
        copy(d, 2).start()
    yield "tail"
    for k in (1, 2):
        for d in range(2):
            arrived(d, k).wait_recv()
    for k in range(3):
        for d in range(2):
            late.append(functools.partial(copy, d, k))


def kernel(
    hid, again, q, lens, block_owner, fgain, kvw_h, cache_h, wout_h, vocab_h,
    lay_out, ent,
    lay, kvw, cache, wv, vv, kvbuf, qs, m1, l1, o1, abuf, psend, precv, xs, xr, own, hpart, fin,
    *rest,
):
    bufs = rest[:len(PARTS)]
    (
        acc, ssq, st1, st2,
        lsem, csem, kvs_sem, kvr_sem, vsem, hs_sem, hr_sem, as_sem, ar_sem, ays_sem, ayr_sem, fs_sem, fr_sem,
        ps_sem, xs_sem, xr_sem,
        uni_s, uni_r, mid_s, mid_r, p4s, p4r, p8s, p8r, ls_sem, lr_sem, core_sem, t1s, t1r, t2s, t2r, es_sem,
    ) = rest[len(PARTS):]
    me = Place()
    decode, prefill = me.decode, me.prefill
    x, y, z, c, yh, h, r = me.x, me.y, me.z, me.c, me.yh, me.h, me.r
    d_model = hid.shape[1]
    late = []
    near = wrap(jnp.where(decode, y + 1, y - 1), NY)
    home_y = jnp.where(decode, near, y)
    holder = c == lax.rem(z, 2)
    xz = lax.div(z, 2)

    cache_copies = [
        pltpu.make_async_copy(
            cache_h.at[pl.ds(i * 4, 4)], cache.at[pl.ds(i * 4, 4)], csem.at[i]
        )
        for i in range(CACHE_PARTS)
    ]
    step = d_model // KV_PARTS
    kv_copies = [
        pltpu.make_async_copy(
            kvw_h.at[pl.ds(i * step, step)], kvw.at[pl.ds(i * step, step)], lsem.at[i]
        )
        for i in range(KV_PARTS)
    ]
    w_copy = pltpu.make_async_copy(wout_h, wv, lsem.at[KV_PARTS])
    v_copy = pltpu.make_async_copy(vocab_h, vv.at[0], lsem.at[KV_PARTS + 1])
    for cp in kv_copies:
        cp.start()

    @pl.when(decode)
    def _():
        for cp in cache_copies:
            cp.start()

    w_copy.start()
    v_copy.start()

    @pl.when(prefill)
    def _():
        kvbuf[...] = jnp.zeros_like(kvbuf)

    peers = [dict(dz=k) for k in range(1, NZ)]
    peers += [dict(dy=2, dz=k) for k in range(1, NZ)]
    peers += [dict(dx=i, dy=j) for i in range(NX) for j in range(NY) if i or j]
    peers += [dict(dc=1, dz=k) for k in range(NZ)]
    barrier = pltpu.get_barrier_semaphore()
    for p in peers:
        pl.semaphore_signal(barrier, 1, device_id=me.off(**p), device_id_type=MESH)
    for k in range(1, NZ):
        to = me.at(x, near, wrap(z + k, NZ), c)
        pl.semaphore_signal(barrier, 1, device_id=to, device_id_type=MESH)

    @pl.when(prefill & holder)
    def _():
        for k in range(NZ):
            zz = wrap(z + k, NZ)
            pl.semaphore_signal(barrier, 1, device_id=me.at(xz, near, zz, c), device_id_type=MESH)
            if k:
                pl.semaphore_signal(barrier, 1, device_id=me.at(xz, y, zz, c), device_id_type=MESH)

        @pl.when(x != xz)
        def _():
            pl.semaphore_signal(barrier, 1, device_id=me.at(xz, y, z, c), device_id_type=MESH)

    def square(i, total):
        w = hid[:, pl.ds(pl.multiple_of(i * 1024, 1024), 1024)].astype(F32)
        return total + jnp.sum(w * w, axis=1, keepdims=True)

    total = lax.fori_loop(0, d_model // 1024, square, jnp.zeros((TOK, 1), F32))
    inv = lax.rsqrt(total / d_model + EPS)
    fresh = jnp.zeros((TOK, 256), F32)
    for i in range(KV_PARTS):
        kv_copies[i].wait()

        def part(j, sum_, i=i):
            at = pl.ds(pl.multiple_of(i * step + j * 512, 512), 512)
            n = (hid[:, at].astype(F32) * inv * again[:, at]).astype(BF)
            return sum_ + dot(n, kvw[at, :])

        fresh = lax.fori_loop(0, step // 512, part, fresh)
    fresh = fresh.astype(BF)

    for g in range(8):
        qs[pl.ds(g, TOK, stride=8), :] = q[:, g * 128:(g + 1) * 128].astype(F32)
    scale = 1.0 / math.sqrt(128)

    at_home = prefill & (z == h)
    extra = jnp.where(at_home, 3, 4)
    pl.semaphore_wait(barrier, len(peers) + NZ - 1 + extra)

    vocab_swap = remote(vocab_h, vv.at[1], vsem.at[0], vsem.at[1], me.off(dc=1))

    def hidden_part(zz, half):
        return pl.ds(pl.multiple_of(zz * COLS + half * HALF, HALF), HALF)

    def hidden_copy(k, other):
        zz = wrap(z + k, NZ)
        src = hid.at[:, hidden_part(zz, 1 - yh if other else yh)]
        to = me.at(x, near if other else y, zz, c)
        return remote(src, hpart.at[other], hs_sem.at[k, other], hr_sem.at[other], to)

    def send_later_needs():
        vocab_swap.start()

        @pl.when(z == h)
        def _():
            for k in range(NZ):
                if k:
                    hidden_copy(k, 0).start()
                hidden_copy(k, 1).start()
            hpart[0] = hid[:, hidden_part(z, yh)]

    up, down = me.off(dy=1), me.off(dy=-1)

    @pl.when(prefill)
    def _():
        m1[...] = jnp.full_like(m1, NEG)
        l1[...] = jnp.zeros_like(l1)
        o1[...] = jnp.zeros_like(o1)
        kvbuf[r] = fresh
        sent = []
        for n, k in enumerate((1, 7, 2, 6, 3, 5, 4)):
            cp = remote(kvbuf.at[r], kvbuf.at[r], kvs_sem.at[n], kvr_sem.at[r], me.off(dz=k))
            cp.start()
            sent.append(cp)

        def across(k):
            return remote(kvbuf.at[r], kvbuf.at[r], kvs_sem.at[23 + k], kvr_sem.at[r],
                          me.off(dz=k, dy=2))

        across(0).start()
        for k in range(1, NZ):
            @pl.when(z + k < NZ)
            def _(k=k):
                across(k).start()

        n = 7
        for k in (0, 1, 7, 2, 6, 3, 5, 4):
            i = wrap(z + k, NZ) * 2 + yh
            ref, sem = kvbuf.at[i], kvr_sem.at[i]
            if k:
                remote(ref, ref, kvs_sem.at[n], sem, up).wait_recv()
            for to in (up, down):
                cp = remote(ref, ref, kvs_sem.at[n], sem, to)
                cp.start()
                sent.append(cp)
                n += 1
        send_later_needs()
        for k in range(NZ):
            @pl.when(k <= z)
            def _(k=k):
                i = k * 2 + 1 - yh
                remote(kvbuf.at[i], kvbuf.at[i], kvs_sem.at[0], kvr_sem.at[i], up).wait_recv()

        for cp in sent:
            cp.wait_send()
        across(0).wait_send()
        for k in range(1, NZ):
            @pl.when(z + k < NZ)
            def _(k=k):
                across(k).wait_send()

    @pl.when(decode)
    def _():
        send_later_needs()
        cache_len = cache.shape[1]

        def rows(first):
            parts = []
            for j in range(4):
                i = first + j
                qi = qs[pl.ds(pl.multiple_of(i * 8, 8), 8), :].astype(BF)
                s = dot_t(qi, cache[i, :, 0:128]) * scale
                at = lax.broadcasted_iota(jnp.int32, (8, cache_len), 1)
                parts.append(jnp.where(at < lens[i], s, NEG))
            s = jnp.concatenate(parts, axis=0)
            top = jnp.max(s, axis=1, keepdims=True)
            p = jnp.exp(s - top)
            total = jnp.sum(p, axis=1, keepdims=True)
            pb = p.astype(BF)
            where = pl.ds(pl.multiple_of(first * 8, 32), 32)
            m1[where, :] = jnp.broadcast_to(top, (32, 128))
            l1[where, :] = jnp.broadcast_to(total, (32, 128))
            out = [dot(pb[8 * j:8 * j + 8], cache[first + j, :, 128:256]) for j in range(4)]
            o1[where, :] = jnp.concatenate(out, axis=0)

        for i in range(CACHE_PARTS):
            cache_copies[i].wait()
            rows(i * 4)
        for i in range(16):
            remote(kvbuf.at[i], kvbuf.at[i], kvs_sem.at[0], kvr_sem.at[i], up).wait_recv()

    keys = kvbuf[:, :, 0:128].reshape(16 * TOK, 128)
    vals = kvbuf[:, :, 128:256].reshape(16 * TOK, 128)
    own_key = fresh[:, 0:128].astype(F32)
    own_val = fresh[:, 128:256].astype(F32)
    flag = jnp.where(decode, 1, 0)
    n_block = block_owner.shape[1]
    digits = jnp.broadcast_to(block_owner[...], (8, n_block))
    spread = lax.broadcasted_iota(jnp.int32, (n_block, n_block * BLK), 1) // BLK
    spread = spread == lax.broadcasted_iota(jnp.int32, (n_block, n_block * BLK), 0)
    spread = spread.astype(F32).astype(BF)
    high = dot((digits >> 4).astype(F32).astype(BF), spread)
    low = dot((digits & 15).astype(F32).astype(BF), spread)
    owners = (high[0:1] * 16.0 + low[0:1]).astype(jnp.int32)

    def a_block(zz, plane, part):
        return abuf.at[lax.rem(zz, 2), part, lax.div(zz, 2), plane]

    def share(k, part):
        zz = wrap(z + k, NZ)
        to = me.at(x, near, z, c)
        return remote(a_block(zz, 0, part), a_block(zz, 1, part),
                      ays_sem.at[part, k % NZ], ayr_sem.at[part, zz], to)

    def first(d, k, part):
        ref = a_block(z, 0, part)
        return remote(ref, ref, as_sem.at[part, d, k - 1], ar_sem.at[part, d, k - 1],
                      me.off(dz=k * (1 - 2 * d)))

    def first_came(d, k, part):
        ref = a_block(wrap(z - k * (1 - 2 * d), NZ), 0, part)
        return remote(ref, ref, as_sem.at[part, d, k - 1], ar_sem.at[part, d, k - 1], me.off(dz=1))

    def piece(zz, plane, part, d, k):
        ref = a_block(zz, plane, part)
        return ref.at[pl.ds(d * 16, 16)] if k == 2 else ref

    def onward(d, k, plane, part):
        sign = 1 - 2 * d
        zz = wrap(z - 2 * sign, NZ)
        to = me.at(x, near if plane else y, wrap(z + k * sign, NZ), c)
        return remote(piece(zz, 0, part, d, k), piece(zz, plane, part, d, k),
                      fs_sem.at[part, plane, d, k - 1], fr_sem.at[part, plane, d, k - 1], to)

    def onward_came(d, k, plane, part):
        zz = wrap(z - (2 + k) * (1 - 2 * d), NZ)
        ref = piece(zz, plane, part, d, k)
        return remote(ref, ref, fs_sem.at[part, plane, d, k - 1],
                      fr_sem.at[part, plane, d, k - 1], me.off(dz=1))

    def a_ring(part):
        def go(make, *what):
            make(*what, part).start()
            late.append(functools.partial(make, *what, part))

        for d in range(2):
            go(first, d, 2)
        go(share, 0)
        for d in range(2):
            go(first, d, 1)
        yield
        for d in range(2):
            first_came(d, 2, part).wait_recv()
            for k, plane in ((2, 1), (2, 0), (1, 1), (1, 0)):
                go(onward, d, k, plane)
        yield
        for d in range(2):
            first_came(d, 1, part).wait_recv()
            go(share, 2 * d - 1)
            go(share, 4 * d - 2)
        yield "last"
        for plane in range(2):
            for d in range(2):
                for k in (1, 2):
                    onward_came(d, k, plane, part).wait_recv()
        for k in (0, 1, -1, 2, -2):
            share(k, part).wait_recv()

    rings = []

    for half in range(2):
        heads = range(half * 4, half * 4 + 4)
        qh = jnp.concatenate([q[:, g * 128:(g + 1) * 128] for g in heads], axis=0)
        s = dot_t(qh, keys) * scale
        row = r * TOK + lax.rem(lax.broadcasted_iota(jnp.int32, s.shape, 0), TOK)
        tok = lax.broadcasted_iota(jnp.int32, s.shape, 1)
        off = flag * jnp.abs(owners - row) + (1 - flag) * jnp.maximum(tok - row, 0)
        s = jnp.where(off == 0, s, NEG)
        mc = jnp.concatenate([m1[pl.ds(g, TOK, stride=8), :] for g in heads], axis=0)
        lc = jnp.concatenate([l1[pl.ds(g, TOK, stride=8), :] for g in heads], axis=0)
        oc = jnp.concatenate([o1[pl.ds(g, TOK, stride=8), :] for g in heads], axis=0)
        ok = jnp.concatenate([own_key] * 4, axis=0)
        ov = jnp.concatenate([own_val] * 4, axis=0)
        so = jnp.sum(qh.astype(F32) * ok, axis=1, keepdims=True) * scale
        so = jnp.where(jnp.broadcast_to(flag, so.shape) == 1, so, NEG)
        mc, lc = mc[:, 0:1], lc[:, 0:1]
        top = jnp.maximum(jnp.maximum(jnp.max(s, axis=1, keepdims=True), mc), so)
        p = jnp.exp(s - top)
        fac = jnp.exp(mc - top)
        po = jnp.exp(so - top)
        total = jnp.sum(p, axis=1, keepdims=True) + lc * fac + po
        out = dot(p.astype(BF), vals) + oc * fac + po.astype(BF).astype(F32) * ov
        out = (out / total).astype(BF)
        for j, g in enumerate(heads):
            a_block(z, 0, half)[:, j * 128:(j + 1) * 128] = out[j * TOK:(j + 1) * TOK]
        rings.append(a_ring(half))
        next(rings[-1])

    drain(*rings)
    w_copy.wait()

    def project(parity):
        rows = [abuf[parity, part].reshape(8 * TOK, HALF) for part in range(2)]
        total = dot(rows[0], wv[0:HALF, :]) + dot(rows[1], wv[HALF:COLS, :])
        return total.reshape(NX, 2, TOK, HALF)

    psend[...] = project(1 - c).astype(BF)
    swap = remote(psend, precv, ps_sem.at[0], ps_sem.at[1], me.off(dc=1))
    swap.start()
    total = project(c)
    swap.wait_recv()
    total = total + precv[...].astype(F32)
    xs[...] = total.astype(BF)
    sends = []
    for k in (2, 1, 3):
        to = wrap(x + k, NX)
        cp = remote(xs.at[to], xr.at[k - 1], xs_sem.at[k - 1], xr_sem.at[k - 1], me.at(to, y, z, c))
        cp.start()
        sends.append(cp)
    for i in range(NX):
        @pl.when(x == i)
        def _(i=i):
            own[...] = total[i]

    @pl.when(z != h)
    def _():
        hidden_copy(0, 0).wait_recv()

    hidden_copy(0, 1).wait_recv()
    rows_out = own[...] + hpart[...].astype(F32)
    for cp in sends:
        cp.wait_recv()
    for k in range(3):
        rows_out = rows_out + xr[k].astype(F32)
    fin[...] = rows_out.astype(BF)

    rows_d = fin[1 - me.s]
    strip = jnp.concatenate([rows_d[0:16], rows_d[16:32]], axis=1)
    spot = {"x": x, "y": y, "z": z}
    for (order, lo, hi), buf in zip(PARTS, bufs):
        buf[tuple(spot[a] for a in reversed(order))] = strip[:, lo:hi]

    def way(p):
        order, lo, hi = PARTS[p]
        buf = bufs[p]
        a1, a2, a3 = order
        i2, i3 = spot[a2], spot[a3]
        n2 = buf.shape[1]
        yield from unicast(me, "d" + a1, lambda i: buf.at[i3, i2, i], uni_s.at[p], uni_r.at[p], late)
        yield from unicast(me, "d" + a2, lambda i: buf.at[i3, i], mid_s.at[p], mid_r.at[p], late)
        if a3 == "z":
            yield from last(ring8_halves(
                me, lambda i, k: buf.at[i, pl.ds(k * (n2 // 2), n2 // 2)],
                p8s.at[p], p8r.at[p], late))
        else:
            yield from last(ring4(
                me, "d" + a3, lambda i, k: buf.at[i, pl.ds(k * (n2 // 2), n2 // 2)],
                p4s.at[p], p4r.at[p], late))

    def owner_cols(zz, half):
        return lay.at[:, pl.ds(pl.multiple_of(zz * COLS + half * HALF, HALF), HALF)]

    def owner_copy(k):
        n = z * 2 + yh
        to = me.at(wrap(x + k, NX), home_y, h, c)
        return remote(fin.at[me.s], owner_cols(z, yh), ls_sem.at[k], lr_sem.at[n], to)

    core_copy = remote(lay, lay, core_sem.at[0], core_sem.at[1], me.off(dc=1))

    def prefill_rows():
        for k in (2, 1, 3):
            owner_copy(k).start()

        @pl.when(jnp.logical_not(at_home))
        def _():
            owner_copy(0).start()

        @pl.when(at_home)
        def _():
            owner_cols(z, yh)[...] = fin[0]

        yield

    drain(*[way(p) for p in range(len(PARTS))], prefill_rows())


    @pl.when(prefill & holder)
    def _():
        for k in range(NZ):
            zz = wrap(z + k, NZ)
            for half in (yh, 1 - yh):
                def wait(zz=zz, half=half):
                    ref = owner_cols(zz, half)
                    remote(ref, ref, ls_sem.at[0], lr_sem.at[zz * 2 + half], up).wait_recv()
                if k == 0 and half is yh:
                    pl.when(x != xz)(wait)
                else:
                    wait()

    def held(i_x, i_y, i_z):
        at = {"x": i_x, "y": i_y, "z": i_z}
        pieces = {}
        for (order, lo, hi), buf in zip(PARTS, bufs):
            pieces[lo] = buf[tuple(at[a] for a in reversed(order))]
        line = jnp.concatenate([pieces[lo] for lo in sorted(pieces)], axis=1)
        return line[:, 0:HALF], line[:, HALF:COLS]

    @pl.when(decode & holder)
    def _():
        for zz in range(NZ):
            for half in range(2):
                i_y = jnp.where(yh == half, 2 * yh + 1, 2 * half)
                low, high = held(xz, i_y, zz)
                at = zz * COLS + half * HALF
                lay[0:16, at:at + HALF] = low
                lay[16:32, at:at + HALF] = high

    out_copy = pltpu.make_async_copy(lay, lay_out, es_sem)

    @pl.when(holder)
    def _():
        core_copy.start()
        out_copy.start()

    v_copy.wait()
    vocab_swap.wait_recv()
    acc[...] = jnp.zeros_like(acc)
    ssq[...] = jnp.zeros_like(ssq)

    def block(zz, carry):
        base = pl.multiple_of(zz * COLS, COLS)
        for half in range(2):
            rows = []
            for i_x in range(NX):
                for plane in range(2):
                    rows += held(i_x, 2 * plane + 1 if half == plane else 2 * half, zz)
            rows = jnp.concatenate(rows, axis=0).astype(F32)
            at = pl.ds(base + half * HALF, HALF)
            sq = rows * rows
            ssq[...] += sq[:, 0:128] + sq[:, 128:256] + sq[:, 256:384] + sq[:, 384:512]
            gained = (rows * fgain[:, at]).astype(BF)
            for k in range(2):
                acc[:, k * 256:(k + 1) * 256] += dot(gained, vv[k, at, :])
        return carry

    lax.fori_loop(0, NZ, block, 0)
    inv = lax.rsqrt(jnp.sum(ssq[...], axis=1, keepdims=True) / d_model + EPS)
    logits = acc[...] * inv
    top = jnp.max(logits, axis=1, keepdims=True)
    shifted = logits - top
    e = jnp.exp(shifted)
    mass = jnp.sum(e, axis=1, keepdims=True)
    moment = jnp.sum(e * shifted, axis=1, keepdims=True)
    lane = lax.broadcasted_iota(jnp.int32, (256, 128), 1)
    packed = jnp.where(lane == 0, top, jnp.where(lane == 1, mass, moment))
    here = x * NY + y
    lines = jnp.transpose(packed)
    st1[here] = jnp.concatenate(
        [lines[i:i + 1, j * 128:(j + 1) * 128] for i in (0, 1, 2, 2) for j in range(2)], axis=0)

    def merge(ref, n):
        tops = [ref[i, 0:2, :] for i in range(n)]
        best = tops[0]
        for t in tops[1:]:
            best = jnp.maximum(best, t)
        mass = jnp.zeros_like(best)
        moment = jnp.zeros_like(best)
        for i in range(n):
            gap = tops[i] - best
            f = jnp.exp(gap)
            mass = mass + f * ref[i, 2:4, :]
            moment = moment + f * (ref[i, 4:6, :] + gap * ref[i, 2:4, :])
        return best, mass, moment

    sent = []
    for i in (2, 1, 3, 0):
        for j in (2, 1, 3, 0):
            n = i * NY + j
            if n:
                cp = remote(st1.at[here], st1.at[here], t1s.at[n], t1r.at[here], me.off(dx=i, dy=j))
                cp.start()
                sent.append(cp)
    @pl.when(jnp.logical_not(holder))
    def _():
        core_copy.wait_recv()
        out_copy.start()

    for i in range(NX):
        for j in range(NY):
            if i or j:
                n = wrap(x + i, NX) * NY + wrap(y + j, NY)
                remote(st1.at[n], st1.at[n], t1s.at[0], t1r.at[n], up).wait_recv()
    best, mass, moment = merge(st1, 16)
    st2[c, z] = jnp.concatenate([best, mass, moment, moment], axis=0)

    def totals(k, other):
        return remote(st2.at[c, z], st2.at[c, z], t2s.at[k, other], t2r.at[c, z],
                      me.off(dz=k, dc=other))

    last_step = [(k, j) for k in (4, 3, 5, 2, 6, 1, 7, 0) for j in (0, 1) if k or j]
    for k, j in last_step:
        totals(k, j).start()

    for i in range(NZ):
        for j in range(2):
            at = 1 - c if j else c
            n = wrap(z + i, NZ)
            if i or j:
                remote(st2.at[at, n], st2.at[at, n], t2s.at[0, 0], t2r.at[at, n], up).wait_recv()
    sides = []
    for j in range(2):
        best, mass, moment = merge(st2.at[j], NZ)
        sides.append(jnp.log(mass) - moment / mass)
    for i in range(NX):
        at = (i % 2) * 64
        ent[i:i + 1, :] = jnp.concatenate(
            [side[i // 2:i // 2 + 1, at:at + 64] for side in sides], axis=1)
    out_copy.wait()

    @pl.when(holder)
    def _():
        core_copy.wait_send()

    for k in (1, 2, 3):
        owner_copy(k).wait_send()

    @pl.when(jnp.logical_not(at_home))
    def _():
        owner_copy(0).wait_send()

    @pl.when(z == h)
    def _():
        for k in range(NZ):
            if k:
                hidden_copy(k, 0).wait_send()
            hidden_copy(k, 1).wait_send()

    for make in late:
        make().wait_send()
    for k, j in last_step:
        totals(k, j).wait_send()
    for cp in sends + sent + [swap, vocab_swap]:
        cp.wait_send()


def ring8_halves(me, half, ssem, rsem, late):
    z = me.z

    def copy(d, k, j):
        ref = half(wrap(z - k, NZ) if d == 0 else wrap(z + k, NZ), d if j == 0 else 1 - d)
        return remote(ref, ref, ssem.at[d, k, j], rsem.at[d, k, j], me.off(dz=1 - 2 * d))

    def arrived(d, k, j):
        ref = half(wrap(z - 1 - k, NZ) if d == 0 else wrap(z + 1 + k, NZ), d if j == 0 else 1 - d)
        return remote(ref, ref, ssem.at[d, k, j], rsem.at[d, k, j], me.off(dz=1))

    for j in range(2):
        for d in range(2):
            copy(d, 0, j).start()
    for k in range(1, 4):
        for j in range(2):
            yield
            for d in range(2):
                arrived(d, k - 1, j).wait_recv()
                if k < 3 or j == 0:
                    copy(d, k, j).start()
    yield "tail"
    for d in range(2):
        arrived(d, 3, 0).wait_recv()
    for k in range(4):
        for j in range(2 if k < 3 else 1):
            for d in range(2):
                late.append(functools.partial(copy, d, k, j))


def drain(*steps):
    live, ends = list(steps), []
    while live:
        going = []
        for s in live:
            told = next(s, "end")
            if told == "last":
                ends.append(s)
            elif told != "end":
                going.append(s)
        live = going
    for s in ends:
        for _ in s:
            pass


def last(steps):
    for told in steps:
        yield "last" if told == "tail" else told


def body(hidden, attn_gain, kv_weight, queries, cache_kv, lengths, block_owner, out_weight,
         final_gain, vocab_weight):
    d_model = hidden.shape[2]
    vmem = pl.BlockSpec(memory_space=pltpu.VMEM)
    smem = pl.BlockSpec(memory_space=pltpu.SMEM)
    hbm = pl.BlockSpec(memory_space=pl.ANY)
    dma = pltpu.SemaphoreType.DMA
    size = {"x": NX, "y": NY, "z": NZ}
    spread = [
        pltpu.VMEM(tuple(size[a] for a in reversed(order)) + (16, hi - lo), BF)
        for order, lo, hi in PARTS
    ]
    n = len(PARTS)
    lay, ent = pl.pallas_call(
        kernel,
        out_shape=(
            jax.ShapeDtypeStruct((TOK, d_model), BF),
            jax.ShapeDtypeStruct((NX, 128), F32),
        ),
        in_specs=[vmem, vmem, vmem, smem, vmem, vmem, hbm, hbm, hbm, hbm],
        out_specs=(hbm, vmem),
        scratch_shapes=[
            pltpu.VMEM((TOK, d_model), BF),
            pltpu.VMEM(kv_weight.shape, BF),
            pltpu.VMEM(cache_kv.shape, BF),
            pltpu.VMEM(out_weight.shape, BF),
            pltpu.VMEM((2,) + vocab_weight.shape, BF),
            pltpu.VMEM((16, TOK, 256), BF),
            pltpu.VMEM((256, 128), F32),
            pltpu.VMEM((256, 128), F32),
            pltpu.VMEM((256, 128), F32),
            pltpu.VMEM((256, 128), F32),
            pltpu.VMEM((2, 2, NX, 2, TOK, HALF), BF),
            pltpu.VMEM((NX, 2, TOK, HALF), BF),
            pltpu.VMEM((NX, 2, TOK, HALF), BF),
            pltpu.VMEM((NX, 2, TOK, HALF), BF),
            pltpu.VMEM((3, 2, TOK, HALF), BF),
            pltpu.VMEM((2, TOK, HALF), F32),
            pltpu.VMEM((2, TOK, HALF), BF),
            pltpu.VMEM((2, TOK, HALF), BF),
            *spread,
            pltpu.VMEM((256, 512), F32),
            pltpu.VMEM((256, 128), F32),
            pltpu.VMEM((16, 8, 128), F32),
            pltpu.VMEM((2, NZ, 8, 128), F32),
            dma((KV_PARTS + 2,)),
            dma((CACHE_PARTS,)),
            dma((31,)),
            dma((16,)),
            dma((2,)),
            dma((NZ, 2)),
            dma((2,)),
            dma((2, 2, 2)),
            dma((2, 2, 2)),
            dma((2, NZ)),
            dma((2, NZ)),
            dma((2, 2, 2, 2)),
            dma((2, 2, 2, 2)),
            dma((2,)),
            dma((3,)),
            dma((3,)),
            dma((n, NZ)),
            dma((n, NZ)),
            dma((n, NZ)),
            dma((n, NZ)),
            dma((n, 2, 3)),
            dma((n, 2, 3)),
            dma((n, 2, 4, 2)),
            dma((n, 2, 4, 2)),
            dma((4,)),
            dma((16,)),
            dma((2,)),
            dma((16,)),
            dma((16,)),
            dma((NZ, 2)),
            dma((2, NZ)),
            dma,
        ],
        compiler_params=pltpu.CompilerParams(
            collective_id=0, has_side_effects=True, vmem_limit_bytes=56 * 1024 * 1024
        ),
        cost_estimate=pl.CostEstimate(
            flops=4_000_000_000, bytes_accessed=24_000_000, transcendentals=1_000_000
        ),
        name="step",
    )(hidden[0], attn_gain[None, :], queries[0], lengths, block_owner[None, :], final_gain[None, :],
      kv_weight, cache_kv, out_weight, vocab_weight)
    return (lay[None], ent.reshape(512))


def solution(mesh):
    return jax.shard_map(
        body,
        mesh=mesh,
        in_specs=(
            P("section", "row", None),
            P(),
            P(None, "head"),
            P("section", "row", "head"),
            P("row", None, "head"),
            P("row"),
            P(),
            P("head", "row"),
            P(),
            P(None, ("section", "head", "row")),
        ),
        out_specs=(P("section", "row", None), P()),
        check_vma=False,
    )
```

```python
import functools
import math

import jax
import jax.numpy as jnp
from jax import lax
from jax.experimental import pallas as pl
from jax.experimental.pallas import tpu as pltpu
from jax.sharding import PartitionSpec as P

MESH = pl.DeviceIdType.MESH
BF = jnp.bfloat16
F32 = jnp.float32
EPS = 1e-05
NEG = -1e30
BLK = 4
NX, NY, NZ = 4, 4, 8
TOK = 32
COLS = 1024
CACHE_PARTS = 8
KV_PARTS = 4
HALF = 512
PARTS = (("yxz", 0, 384), ("zyx", 384, 768), ("zxy", 768, 1024))


def dot(a, b):
    return jnp.dot(a, b, preferred_element_type=F32)


def dot_t(a, b):
    return lax.dot_general(a, b, (((1,), (1,)), ((), ())), preferred_element_type=F32)


def wrap(value, n):
    return lax.rem(value + n, n)


class Place:
    def __init__(self):
        s, h, r = (lax.axis_index(a) for a in ("section", "head", "row"))
        self.s, self.h, self.r = s, h, r
        self.x, self.c = lax.div(h, 2), lax.rem(h, 2)
        self.z, self.yh = lax.div(r, 2), lax.rem(r, 2)
        self.y = self.yh * 2 + s
        self.decode = s == 1
        self.prefill = s == 0

    def at(self, x, y, z, c):
        return (lax.rem(y, 2), x * 2 + c, z * 2 + lax.div(y, 2))

    def on(self, axis):
        return {"dx": (self.x, NX), "dy": (self.y, NY), "dz": (self.z, NZ)}[axis]

    def off(self, dx=0, dy=0, dz=0, dc=0):
        x = wrap(self.x + dx, NX) if dx else self.x
        y = wrap(self.y + dy, NY) if dy else self.y
        z = wrap(self.z + dz, NZ) if dz else self.z
        c = 1 - self.c if dc else self.c
        return self.at(x, y, z, c)


def remote(src, dst, ssem, rsem, device):
    return pltpu.make_async_remote_copy(
        src_ref=src, dst_ref=dst, send_sem=ssem, recv_sem=rsem,
        device_id=device, device_id_type=MESH,
    )


def unicast(me, axis, block, ssem, rsem, late):
    at, n = me.on(axis)

    def copy(k):
        ref = block(at)
        return remote(ref, ref, ssem.at[k], rsem.at[at], me.off(**{axis: k}))

    order = [k for d in range(n // 2, 0, -1) for k in sorted({d, n - d})]
    for k in order:
        copy(k).start()
        late.append(functools.partial(copy, k))
    yield
    for k in reversed(order):
        source = wrap(at + k, n)
        ref = block(source)
        remote(ref, ref, ssem.at[0], rsem.at[source], me.off(**{axis: 1})).wait_recv()


def ring4(me, axis, half, ssem, rsem, late):
    at, n = me.on(axis)

    def copy(d, k):
        ref = half(at, d if k == 0 else 1 - d) if k < 2 else half(wrap(at - 1 + 2 * d, n), d)
        return remote(ref, ref, ssem.at[d, k], rsem.at[d, k], me.off(**{axis: 1 - 2 * d}))

    def arrived(d, k):
        near = wrap(at - 1 + 2 * d, n)
        ref = half(near, d if k == 0 else 1 - d) if k < 2 else half(wrap(at + 2, n), d)
        return remote(ref, ref, ssem.at[d, k], rsem.at[d, k], me.off(**{axis: 1}))

    for k in range(2):
        for d in range(2):
            copy(d, k).start()
    yield
    for d in range(2):
        arrived(d, 0).wait_recv()
        copy(d, 2).start()
    yield "tail"
    for k in (1, 2):
        for d in range(2):
            arrived(d, k).wait_recv()
    for k in range(3):
        for d in range(2):
            late.append(functools.partial(copy, d, k))


def kernel(
    hid, again, q, lens, block_owner, fgain, kvw_h, cache_h, wout_h, vocab_h,
    lay_out, ent,
    lay, kvw, cache, wv, vv, kvbuf, qs, m1, l1, o1, abuf, psend, precv, xs, xr, own, hpart, fin,
    *rest,
):
    bufs = rest[:len(PARTS)]
    (
        acc, ssq, st1, st2,
        lsem, csem, kvs_sem, kvr_sem, vsem, hs_sem, hr_sem, as_sem, ar_sem, ays_sem, ayr_sem, fs_sem, fr_sem,
        ps_sem, xs_sem, xr_sem,
        uni_s, uni_r, mid_s, mid_r, p4s, p4r, p8s, p8r, ls_sem, lr_sem, core_sem, t1s, t1r, t2s, t2r, es_sem,
    ) = rest[len(PARTS):]
    me = Place()
    decode, prefill = me.decode, me.prefill
    x, y, z, c, yh, h, r = me.x, me.y, me.z, me.c, me.yh, me.h, me.r
    d_model = hid.shape[1]
    late = []
    near = wrap(jnp.where(decode, y + 1, y - 1), NY)
    home_y = jnp.where(decode, near, y)
    holder = c == lax.rem(z, 2)
    xz = lax.div(z, 2)

    cache_copies = [
        pltpu.make_async_copy(
            cache_h.at[pl.ds(i * 4, 4)], cache.at[pl.ds(i * 4, 4)], csem.at[i]
        )
        for i in range(CACHE_PARTS)
    ]
    step = d_model // KV_PARTS
    kv_copies = [
        pltpu.make_async_copy(
            kvw_h.at[pl.ds(i * step, step)], kvw.at[pl.ds(i * step, step)], lsem.at[i]
        )
        for i in range(KV_PARTS)
    ]
    w_copy = pltpu.make_async_copy(wout_h, wv, lsem.at[KV_PARTS])
    v_copy = pltpu.make_async_copy(vocab_h, vv.at[0], lsem.at[KV_PARTS + 1])
    for cp in kv_copies:
        cp.start()

    @pl.when(decode)
    def _():
        for cp in cache_copies:
            cp.start()

    w_copy.start()
    v_copy.start()

    @pl.when(prefill)
    def _():
        kvbuf[...] = jnp.zeros_like(kvbuf)

    peers = [dict(dz=k) for k in range(1, NZ)]
    peers += [dict(dy=2, dz=k) for k in range(1, NZ)]
    peers += [dict(dx=i, dy=j) for i in range(NX) for j in range(NY) if i or j]
    peers += [dict(dc=1, dz=k) for k in range(NZ)]
    barrier = pltpu.get_barrier_semaphore()
    for p in peers:
        pl.semaphore_signal(barrier, 1, device_id=me.off(**p), device_id_type=MESH)
    for k in range(1, NZ):
        to = me.at(x, near, wrap(z + k, NZ), c)
        pl.semaphore_signal(barrier, 1, device_id=to, device_id_type=MESH)

    @pl.when(prefill & holder)
    def _():
        for k in range(NZ):
            zz = wrap(z + k, NZ)
            pl.semaphore_signal(barrier, 1, device_id=me.at(xz, near, zz, c), device_id_type=MESH)
            if k:
                pl.semaphore_signal(barrier, 1, device_id=me.at(xz, y, zz, c), device_id_type=MESH)

        @pl.when(x != xz)
        def _():
            pl.semaphore_signal(barrier, 1, device_id=me.at(xz, y, z, c), device_id_type=MESH)

    def square(i, total):
        w = hid[:, pl.ds(pl.multiple_of(i * 1024, 1024), 1024)].astype(F32)
        return total + jnp.sum(w * w, axis=1, keepdims=True)

    total = lax.fori_loop(0, d_model // 1024, square, jnp.zeros((TOK, 1), F32))
    inv = lax.rsqrt(total / d_model + EPS)
    fresh = jnp.zeros((TOK, 256), F32)
    for i in range(KV_PARTS):
        kv_copies[i].wait()

        def part(j, sum_, i=i):
            at = pl.ds(pl.multiple_of(i * step + j * 1024, 1024), 1024)
            n = (hid[:, at].astype(F32) * inv * again[:, at]).astype(BF)
            return sum_ + dot(n, kvw[at, :])

        fresh = lax.fori_loop(0, step // 1024, part, fresh)
    fresh = fresh.astype(BF)

    for g in range(8):
        qs[pl.ds(g, TOK, stride=8), :] = q[:, g * 128:(g + 1) * 128].astype(F32)
    scale = 1.0 / math.sqrt(128)

    at_home = prefill & (z == h)
    extra = jnp.where(at_home, 3, 4)
    pl.semaphore_wait(barrier, len(peers) + NZ - 1 + extra)

    vocab_swap = remote(vocab_h, vv.at[1], vsem.at[0], vsem.at[1], me.off(dc=1))

    def hidden_part(zz, half):
        return pl.ds(pl.multiple_of(zz * COLS + half * HALF, HALF), HALF)

    def hidden_copy(k, other):
        zz = wrap(z + k, NZ)
        src = hid.at[:, hidden_part(zz, 1 - yh if other else yh)]
        to = me.at(x, near if other else y, zz, c)
        return remote(src, hpart.at[other], hs_sem.at[k, other], hr_sem.at[other], to)

    def send_later_needs():
        vocab_swap.start()

        @pl.when(z == h)
        def _():
            for k in range(NZ):
                if k:
                    hidden_copy(k, 0).start()
                hidden_copy(k, 1).start()
            hpart[0] = hid[:, hidden_part(z, yh)]

    up, down = me.off(dy=1), me.off(dy=-1)

    @pl.when(prefill)
    def _():
        m1[...] = jnp.full_like(m1, NEG)
        l1[...] = jnp.zeros_like(l1)
        o1[...] = jnp.zeros_like(o1)
        kvbuf[r] = fresh
        sent = []
        for n, k in enumerate((1, 7, 2, 6, 3, 5, 4)):
            cp = remote(kvbuf.at[r], kvbuf.at[r], kvs_sem.at[n], kvr_sem.at[r], me.off(dz=k))
            cp.start()
            sent.append(cp)

        def across(k):
            return remote(kvbuf.at[r], kvbuf.at[r], kvs_sem.at[23 + k], kvr_sem.at[r],
                          me.off(dz=k, dy=2))

        across(0).start()
        for k in range(1, NZ):
            @pl.when(z + k < NZ)
            def _(k=k):
                across(k).start()

        n = 7
        for k in (0, 1, 7, 2, 6, 3, 5, 4):
            i = wrap(z + k, NZ) * 2 + yh
            ref, sem = kvbuf.at[i], kvr_sem.at[i]
            if k:
                remote(ref, ref, kvs_sem.at[n], sem, up).wait_recv()
            for to in (up, down):
                cp = remote(ref, ref, kvs_sem.at[n], sem, to)
                cp.start()
                sent.append(cp)
                n += 1
        send_later_needs()
        for k in range(NZ):
            @pl.when(k <= z)
            def _(k=k):
                i = k * 2 + 1 - yh
                remote(kvbuf.at[i], kvbuf.at[i], kvs_sem.at[0], kvr_sem.at[i], up).wait_recv()

        for cp in sent:
            cp.wait_send()
        across(0).wait_send()
        for k in range(1, NZ):
            @pl.when(z + k < NZ)
            def _(k=k):
                across(k).wait_send()

    @pl.when(decode)
    def _():
        send_later_needs()
        cache_len = cache.shape[1]

        def rows(first):
            parts = []
            for j in range(4):
                i = first + j
                qi = qs[pl.ds(pl.multiple_of(i * 8, 8), 8), :].astype(BF)
                s = dot_t(qi, cache[i, :, 0:128]) * scale
                at = lax.broadcasted_iota(jnp.int32, (8, cache_len), 1)
                parts.append(jnp.where(at < lens[i], s, NEG))
            s = jnp.concatenate(parts, axis=0)
            top = jnp.max(s, axis=1, keepdims=True)
            p = jnp.exp(s - top)
            total = jnp.sum(p, axis=1, keepdims=True)
            pb = p.astype(BF)
            where = pl.ds(pl.multiple_of(first * 8, 32), 32)
            m1[where, :] = jnp.broadcast_to(top, (32, 128))
            l1[where, :] = jnp.broadcast_to(total, (32, 128))
            out = [dot(pb[8 * j:8 * j + 8], cache[first + j, :, 128:256]) for j in range(4)]
            o1[where, :] = jnp.concatenate(out, axis=0)

        for i in range(CACHE_PARTS):
            cache_copies[i].wait()
            rows(i * 4)
        for i in range(16):
            remote(kvbuf.at[i], kvbuf.at[i], kvs_sem.at[0], kvr_sem.at[i], up).wait_recv()

    keys = kvbuf[:, :, 0:128].reshape(16 * TOK, 128)
    vals = kvbuf[:, :, 128:256].reshape(16 * TOK, 128)
    own_key = fresh[:, 0:128].astype(F32)
    own_val = fresh[:, 128:256].astype(F32)
    flag = jnp.where(decode, 1, 0)
    n_block = block_owner.shape[1]
    digits = jnp.broadcast_to(block_owner[...], (8, n_block))
    spread = lax.broadcasted_iota(jnp.int32, (n_block, n_block * BLK), 1) // BLK
    spread = spread == lax.broadcasted_iota(jnp.int32, (n_block, n_block * BLK), 0)
    spread = spread.astype(F32).astype(BF)
    high = dot((digits >> 4).astype(F32).astype(BF), spread)
    low = dot((digits & 15).astype(F32).astype(BF), spread)
    owners = (high[0:1] * 16.0 + low[0:1]).astype(jnp.int32)

    def a_block(zz, plane, part):
        return abuf.at[lax.rem(zz, 2), part, lax.div(zz, 2), plane]

    def share(k, part):
        zz = wrap(z + k, NZ)
        to = me.at(x, near, z, c)
        return remote(a_block(zz, 0, part), a_block(zz, 1, part),
                      ays_sem.at[part, k % NZ], ayr_sem.at[part, zz], to)

    def first(d, k, part):
        ref = a_block(z, 0, part)
        return remote(ref, ref, as_sem.at[part, d, k - 1], ar_sem.at[part, d, k - 1],
                      me.off(dz=k * (1 - 2 * d)))

    def first_came(d, k, part):
        ref = a_block(wrap(z - k * (1 - 2 * d), NZ), 0, part)
        return remote(ref, ref, as_sem.at[part, d, k - 1], ar_sem.at[part, d, k - 1], me.off(dz=1))

    def piece(zz, plane, part, d, k):
        ref = a_block(zz, plane, part)
        return ref.at[pl.ds(d * 16, 16)] if k == 2 else ref

    def onward(d, k, plane, part):
        sign = 1 - 2 * d
        zz = wrap(z - 2 * sign, NZ)
        to = me.at(x, near if plane else y, wrap(z + k * sign, NZ), c)
        return remote(piece(zz, 0, part, d, k), piece(zz, plane, part, d, k),
                      fs_sem.at[part, plane, d, k - 1], fr_sem.at[part, plane, d, k - 1], to)

    def onward_came(d, k, plane, part):
        zz = wrap(z - (2 + k) * (1 - 2 * d), NZ)
        ref = piece(zz, plane, part, d, k)
        return remote(ref, ref, fs_sem.at[part, plane, d, k - 1],
                      fr_sem.at[part, plane, d, k - 1], me.off(dz=1))

    def a_ring(part):
        def go(make, *what):
            make(*what, part).start()
            late.append(functools.partial(make, *what, part))

        for d in range(2):
            go(first, d, 2)
        go(share, 0)
        for d in range(2):
            go(first, d, 1)
        yield
        for d in range(2):
            first_came(d, 2, part).wait_recv()
            for k, plane in ((2, 1), (2, 0), (1, 1), (1, 0)):
                go(onward, d, k, plane)
        yield
        for d in range(2):
            first_came(d, 1, part).wait_recv()
            go(share, 2 * d - 1)
            go(share, 4 * d - 2)
        yield "last"
        for plane in range(2):
            for d in range(2):
                for k in (1, 2):
                    onward_came(d, k, plane, part).wait_recv()
        for k in (0, 1, -1, 2, -2):
            share(k, part).wait_recv()

    rings = []

    for half in range(2):
        heads = range(half * 4, half * 4 + 4)
        qh = jnp.concatenate([q[:, g * 128:(g + 1) * 128] for g in heads], axis=0)
        s = dot_t(qh, keys) * scale
        row = r * TOK + lax.rem(lax.broadcasted_iota(jnp.int32, s.shape, 0), TOK)
        tok = lax.broadcasted_iota(jnp.int32, s.shape, 1)
        off = flag * jnp.abs(owners - row) + (1 - flag) * jnp.maximum(tok - row, 0)
        s = jnp.where(off == 0, s, NEG)
        mc = jnp.concatenate([m1[pl.ds(g, TOK, stride=8), :] for g in heads], axis=0)
        lc = jnp.concatenate([l1[pl.ds(g, TOK, stride=8), :] for g in heads], axis=0)
        oc = jnp.concatenate([o1[pl.ds(g, TOK, stride=8), :] for g in heads], axis=0)
        ok = jnp.concatenate([own_key] * 4, axis=0)
        ov = jnp.concatenate([own_val] * 4, axis=0)
        so = jnp.sum(qh.astype(F32) * ok, axis=1, keepdims=True) * scale
        so = jnp.where(jnp.broadcast_to(flag, so.shape) == 1, so, NEG)
        mc, lc = mc[:, 0:1], lc[:, 0:1]
        top = jnp.maximum(jnp.maximum(jnp.max(s, axis=1, keepdims=True), mc), so)
        p = jnp.exp(s - top)
        fac = jnp.exp(mc - top)
        po = jnp.exp(so - top)
        total = jnp.sum(p, axis=1, keepdims=True) + lc * fac + po
        out = dot(p.astype(BF), vals) + oc * fac + po.astype(BF).astype(F32) * ov
        out = (out / total).astype(BF)
        for j, g in enumerate(heads):
            a_block(z, 0, half)[:, j * 128:(j + 1) * 128] = out[j * TOK:(j + 1) * TOK]
        rings.append(a_ring(half))
        next(rings[-1])

    drain(*rings)
    w_copy.wait()

    def project(parity):
        rows = [abuf[parity, part].reshape(8 * TOK, HALF) for part in range(2)]
        total = dot(rows[0], wv[0:HALF, :]) + dot(rows[1], wv[HALF:COLS, :])
        return total.reshape(NX, 2, TOK, HALF)

    psend[...] = project(1 - c).astype(BF)
    swap = remote(psend, precv, ps_sem.at[0], ps_sem.at[1], me.off(dc=1))
    swap.start()
    total = project(c)
    swap.wait_recv()
    total = total + precv[...].astype(F32)
    xs[...] = total.astype(BF)
    sends = []
    for k in (2, 1, 3):
        to = wrap(x + k, NX)
        cp = remote(xs.at[to], xr.at[k - 1], xs_sem.at[k - 1], xr_sem.at[k - 1], me.at(to, y, z, c))
        cp.start()
        sends.append(cp)
    for i in range(NX):
        @pl.when(x == i)
        def _(i=i):
            own[...] = total[i]

    @pl.when(z != h)
    def _():
        hidden_copy(0, 0).wait_recv()

    hidden_copy(0, 1).wait_recv()
    rows_out = own[...] + hpart[...].astype(F32)
    for cp in sends:
        cp.wait_recv()
    for k in range(3):
        rows_out = rows_out + xr[k].astype(F32)
    fin[...] = rows_out.astype(BF)

    rows_d = fin[1 - me.s]
    strip = jnp.concatenate([rows_d[0:16], rows_d[16:32]], axis=1)
    spot = {"x": x, "y": y, "z": z}
    for (order, lo, hi), buf in zip(PARTS, bufs):
        buf[tuple(spot[a] for a in reversed(order))] = strip[:, lo:hi]

    def way(p):
        order, lo, hi = PARTS[p]
        buf = bufs[p]
        a1, a2, a3 = order
        i2, i3 = spot[a2], spot[a3]
        n2 = buf.shape[1]
        yield from unicast(me, "d" + a1, lambda i: buf.at[i3, i2, i], uni_s.at[p], uni_r.at[p], late)
        yield from unicast(me, "d" + a2, lambda i: buf.at[i3, i], mid_s.at[p], mid_r.at[p], late)
        if a3 == "z":
            yield from last(ring8_halves(
                me, lambda i, k: buf.at[i, pl.ds(k * (n2 // 2), n2 // 2)],
                p8s.at[p], p8r.at[p], late))
        else:
            yield from last(ring4(
                me, "d" + a3, lambda i, k: buf.at[i, pl.ds(k * (n2 // 2), n2 // 2)],
                p4s.at[p], p4r.at[p], late))

    def owner_cols(zz, half):
        return lay.at[:, pl.ds(pl.multiple_of(zz * COLS + half * HALF, HALF), HALF)]

    def owner_copy(k):
        n = z * 2 + yh
        to = me.at(wrap(x + k, NX), home_y, h, c)
        return remote(fin.at[me.s], owner_cols(z, yh), ls_sem.at[k], lr_sem.at[n], to)

    core_copy = remote(lay, lay, core_sem.at[0], core_sem.at[1], me.off(dc=1))

    def prefill_rows():
        for k in (2, 1, 3):
            owner_copy(k).start()

        @pl.when(jnp.logical_not(at_home))
        def _():
            owner_copy(0).start()

        @pl.when(at_home)
        def _():
            owner_cols(z, yh)[...] = fin[0]

        yield

    drain(*[way(p) for p in range(len(PARTS))], prefill_rows())


    @pl.when(prefill & holder)
    def _():
        for k in range(NZ):
            zz = wrap(z + k, NZ)
            for half in (yh, 1 - yh):
                def wait(zz=zz, half=half):
                    ref = owner_cols(zz, half)
                    remote(ref, ref, ls_sem.at[0], lr_sem.at[zz * 2 + half], up).wait_recv()
                if k == 0 and half is yh:
                    pl.when(x != xz)(wait)
                else:
                    wait()

    def held(i_x, i_y, i_z):
        at = {"x": i_x, "y": i_y, "z": i_z}
        pieces = {}
        for (order, lo, hi), buf in zip(PARTS, bufs):
            pieces[lo] = buf[tuple(at[a] for a in reversed(order))]
        line = jnp.concatenate([pieces[lo] for lo in sorted(pieces)], axis=1)
        return line[:, 0:HALF], line[:, HALF:COLS]

    @pl.when(decode & holder)
    def _():
        for zz in range(NZ):
            for half in range(2):
                i_y = jnp.where(yh == half, 2 * yh + 1, 2 * half)
                low, high = held(xz, i_y, zz)
                at = zz * COLS + half * HALF
                lay[0:16, at:at + HALF] = low
                lay[16:32, at:at + HALF] = high

    out_copy = pltpu.make_async_copy(lay, lay_out, es_sem)

    @pl.when(holder)
    def _():
        core_copy.start()
        out_copy.start()

    v_copy.wait()
    vocab_swap.wait_recv()
    acc[...] = jnp.zeros_like(acc)
    ssq[...] = jnp.zeros_like(ssq)

    def block(zz, carry):
        base = pl.multiple_of(zz * COLS, COLS)
        for half in range(2):
            rows = []
            for i_x in range(NX):
                for plane in range(2):
                    rows += held(i_x, 2 * plane + 1 if half == plane else 2 * half, zz)
            rows = jnp.concatenate(rows, axis=0).astype(F32)
            at = pl.ds(base + half * HALF, HALF)
            sq = rows * rows
            ssq[...] += sq[:, 0:128] + sq[:, 128:256] + sq[:, 256:384] + sq[:, 384:512]
            gained = (rows * fgain[:, at]).astype(BF)
            for k in range(2):
                acc[:, k * 256:(k + 1) * 256] += dot(gained, vv[k, at, :])
        return carry

    lax.fori_loop(0, NZ, block, 0, unroll=2)
    inv = lax.rsqrt(jnp.sum(ssq[...], axis=1, keepdims=True) / d_model + EPS)
    logits = acc[...] * inv
    top = jnp.max(logits, axis=1, keepdims=True)
    shifted = logits - top
    e = jnp.exp(shifted)
    mass = jnp.sum(e, axis=1, keepdims=True)
    moment = jnp.sum(e * shifted, axis=1, keepdims=True)
    lane = lax.broadcasted_iota(jnp.int32, (256, 128), 1)
    packed = jnp.where(lane == 0, top, jnp.where(lane == 1, mass, moment))
    here = x * NY + y
    lines = jnp.transpose(packed)
    st1[here] = jnp.concatenate(
        [lines[i:i + 1, j * 128:(j + 1) * 128] for i in (0, 1, 2, 2) for j in range(2)], axis=0)

    def merge(ref, n):
        tops = [ref[i, 0:2, :] for i in range(n)]
        best = tops[0]
        for t in tops[1:]:
            best = jnp.maximum(best, t)
        mass = jnp.zeros_like(best)
        moment = jnp.zeros_like(best)
        for i in range(n):
            gap = tops[i] - best
            f = jnp.exp(gap)
            mass = mass + f * ref[i, 2:4, :]
            moment = moment + f * (ref[i, 4:6, :] + gap * ref[i, 2:4, :])
        return best, mass, moment

    sent = []
    for i in (2, 1, 3, 0):
        for j in (2, 1, 3, 0):
            n = i * NY + j
            if n:
                cp = remote(st1.at[here], st1.at[here], t1s.at[n], t1r.at[here], me.off(dx=i, dy=j))
                cp.start()
                sent.append(cp)
    @pl.when(jnp.logical_not(holder))
    def _():
        core_copy.wait_recv()
        out_copy.start()

    for i in range(NX):
        for j in range(NY):
            if i or j:
                n = wrap(x + i, NX) * NY + wrap(y + j, NY)
                remote(st1.at[n], st1.at[n], t1s.at[0], t1r.at[n], up).wait_recv()
    best, mass, moment = merge(st1, 16)
    st2[c, z] = jnp.concatenate([best, mass, moment, moment], axis=0)

    def totals(k, other):
        return remote(st2.at[c, z], st2.at[c, z], t2s.at[k, other], t2r.at[c, z],
                      me.off(dz=k, dc=other))

    last_step = [(k, j) for k in (4, 3, 5, 2, 6, 1, 7, 0) for j in (0, 1) if k or j]
    for k, j in last_step:
        totals(k, j).start()

    for i in range(NZ):
        for j in range(2):
            at = 1 - c if j else c
            n = wrap(z + i, NZ)
            if i or j:
                remote(st2.at[at, n], st2.at[at, n], t2s.at[0, 0], t2r.at[at, n], up).wait_recv()
    sides = []
    for j in range(2):
        best, mass, moment = merge(st2.at[j], NZ)
        sides.append(jnp.log(mass) - moment / mass)
    for i in range(NX):
        at = (i % 2) * 64
        ent[i:i + 1, :] = jnp.concatenate(
            [side[i // 2:i // 2 + 1, at:at + 64] for side in sides], axis=1)
    out_copy.wait()

    @pl.when(holder)
    def _():
        core_copy.wait_send()

    for k in (1, 2, 3):
        owner_copy(k).wait_send()

    @pl.when(jnp.logical_not(at_home))
    def _():
        owner_copy(0).wait_send()

    @pl.when(z == h)
    def _():
        for k in range(NZ):
            if k:
                hidden_copy(k, 0).wait_send()
            hidden_copy(k, 1).wait_send()

    for make in late:
        make().wait_send()
    for k, j in last_step:
        totals(k, j).wait_send()
    for cp in sends + sent + [swap, vocab_swap]:
        cp.wait_send()


def ring8_halves(me, half, ssem, rsem, late):
    z = me.z

    def copy(d, k, j):
        ref = half(wrap(z - k, NZ) if d == 0 else wrap(z + k, NZ), d if j == 0 else 1 - d)
        return remote(ref, ref, ssem.at[d, k, j], rsem.at[d, k, j], me.off(dz=1 - 2 * d))

    def arrived(d, k, j):
        ref = half(wrap(z - 1 - k, NZ) if d == 0 else wrap(z + 1 + k, NZ), d if j == 0 else 1 - d)
        return remote(ref, ref, ssem.at[d, k, j], rsem.at[d, k, j], me.off(dz=1))

    for j in range(2):
        for d in range(2):
            copy(d, 0, j).start()
    for k in range(1, 4):
        for j in range(2):
            yield
            for d in range(2):
                arrived(d, k - 1, j).wait_recv()
                if k < 3 or j == 0:
                    copy(d, k, j).start()
    yield "tail"
    for d in range(2):
        arrived(d, 3, 0).wait_recv()
    for k in range(4):
        for j in range(2 if k < 3 else 1):
            for d in range(2):
                late.append(functools.partial(copy, d, k, j))


def drain(*steps):
    live, ends = list(steps), []
    while live:
        going = []
        for s in live:
            told = next(s, "end")
            if told == "last":
                ends.append(s)
            elif told != "end":
                going.append(s)
        live = going
    for s in ends:
        for _ in s:
            pass


def last(steps):
    for told in steps:
        yield "last" if told == "tail" else told


def body(hidden, attn_gain, kv_weight, queries, cache_kv, lengths, block_owner, out_weight,
         final_gain, vocab_weight):
    d_model = hidden.shape[2]
    vmem = pl.BlockSpec(memory_space=pltpu.VMEM)
    smem = pl.BlockSpec(memory_space=pltpu.SMEM)
    hbm = pl.BlockSpec(memory_space=pl.ANY)
    dma = pltpu.SemaphoreType.DMA
    size = {"x": NX, "y": NY, "z": NZ}
    spread = [
        pltpu.VMEM(tuple(size[a] for a in reversed(order)) + (16, hi - lo), BF)
        for order, lo, hi in PARTS
    ]
    n = len(PARTS)
    lay, ent = pl.pallas_call(
        kernel,
        out_shape=(
            jax.ShapeDtypeStruct((TOK, d_model), BF),
            jax.ShapeDtypeStruct((NX, 128), F32),
        ),
        in_specs=[vmem, vmem, vmem, smem, vmem, vmem, hbm, hbm, hbm, hbm],
        out_specs=(hbm, vmem),
        scratch_shapes=[
            pltpu.VMEM((TOK, d_model), BF),
            pltpu.VMEM(kv_weight.shape, BF),
            pltpu.VMEM(cache_kv.shape, BF),
            pltpu.VMEM(out_weight.shape, BF),
            pltpu.VMEM((2,) + vocab_weight.shape, BF),
            pltpu.VMEM((16, TOK, 256), BF),
            pltpu.VMEM((256, 128), F32),
            pltpu.VMEM((256, 128), F32),
            pltpu.VMEM((256, 128), F32),
            pltpu.VMEM((256, 128), F32),
            pltpu.VMEM((2, 2, NX, 2, TOK, HALF), BF),
            pltpu.VMEM((NX, 2, TOK, HALF), BF),
            pltpu.VMEM((NX, 2, TOK, HALF), BF),
            pltpu.VMEM((NX, 2, TOK, HALF), BF),
            pltpu.VMEM((3, 2, TOK, HALF), BF),
            pltpu.VMEM((2, TOK, HALF), F32),
            pltpu.VMEM((2, TOK, HALF), BF),
            pltpu.VMEM((2, TOK, HALF), BF),
            *spread,
            pltpu.VMEM((256, 512), F32),
            pltpu.VMEM((256, 128), F32),
            pltpu.VMEM((16, 8, 128), F32),
            pltpu.VMEM((2, NZ, 8, 128), F32),
            dma((KV_PARTS + 2,)),
            dma((CACHE_PARTS,)),
            dma((31,)),
            dma((16,)),
            dma((2,)),
            dma((NZ, 2)),
            dma((2,)),
            dma((2, 2, 2)),
            dma((2, 2, 2)),
            dma((2, NZ)),
            dma((2, NZ)),
            dma((2, 2, 2, 2)),
            dma((2, 2, 2, 2)),
            dma((2,)),
            dma((3,)),
            dma((3,)),
            dma((n, NZ)),
            dma((n, NZ)),
            dma((n, NZ)),
            dma((n, NZ)),
            dma((n, 2, 3)),
            dma((n, 2, 3)),
            dma((n, 2, 4, 2)),
            dma((n, 2, 4, 2)),
            dma((4,)),
            dma((16,)),
            dma((2,)),
            dma((16,)),
            dma((16,)),
            dma((NZ, 2)),
            dma((2, NZ)),
            dma,
        ],
        compiler_params=pltpu.CompilerParams(
            collective_id=0, has_side_effects=True, vmem_limit_bytes=56 * 1024 * 1024
        ),
        cost_estimate=pl.CostEstimate(
            flops=4_000_000_000, bytes_accessed=24_000_000, transcendentals=1_000_000
        ),
        name="step",
    )(hidden[0], attn_gain[None, :], queries[0], lengths, block_owner[None, :], final_gain[None, :],
      kv_weight, cache_kv, out_weight, vocab_weight)
    return (lay[None], ent.reshape(512))


def solution(mesh):
    return jax.shard_map(
        body,
        mesh=mesh,
        in_specs=(
            P("section", "row", None),
            P(),
            P(None, "head"),
            P("section", "row", "head"),
            P("row", None, "head"),
            P("row"),
            P(),
            P("head", "row"),
            P(),
            P(None, ("section", "head", "row")),
        ),
        out_specs=(P("section", "row", None), P()),
        check_vma=False,
    )
```
